32 devices in a mesh: dp: 4 (over y, core), frame: 4 (over z), mp: 2 (over x).
Axes of the slice: x: 2, y: 2, z: 4, core: 2. Of those that a mesh axis runs over, the one named last changes fastest.
Arguments:
- projected: bfloat16 [6, 4, 16, 128, 5120], P(None, 'dp', 'frame', None, 'mp'), may hold values from -6 to 6
- codes: float32 [4, 16, 32], P('dp'), may hold values from -6 to 6
- action_weight: float32 [32, 5120], P(None, 'mp'), may hold values from -1 to 1
- clip_ids: int32 [4], replicated, may hold values from 0 to 3, each once
- frame_map: int32 [16], replicated, may hold values from 0 to 15, each once
- segments: int32 [4, 16], P('dp'), may hold values from 0 to 2, never falling along the last dimension, each value on 1 to 8 neighbouring positions
Outputs:
- mixed: bfloat16 [4, 16, 128, 5120], P('dp', 'frame', None, 'mp')
The draws below stay inside these ranges and needn't reach their ends.
Inputs may be any that keep to these rules, and one draw needn't show every extreme that they name: `clip_ids`: each clip id appears once. `frame_map`: each time appears once. `segments`: episode numbers never fall along time.
All inputs are finite; a program needn't handle non-finite values.
Results may differ from the reference program's by a relative error of at most 0.0085.
Values may be sent and summed in bfloat16 or wider, within the bound.
No kernel may reach another device: no remote copies, remote signals or barrier semaphores. Data moves between devices by JAX's collectives and lax.ppermute only.
A program may use at most 128 MiB of HBM per device.

```python
import math
import jax
import jax.numpy as jnp
import numpy as np
from jax import lax

D = 5120
E = 128
F = 16
A = 32
P_SIZE = 128
CLIPS = 4


def draw_projected(key, part):
    key_base = jax.random.fold_in(key, 0)
    shape = (6, CLIPS, F, P_SIZE, D)
    base = jax.random.normal(key_base, shape, jnp.float32)
    spread = jnp.array([1.6, 1.6, 1.0, 1.6, 1.6, 1.0], jnp.float32).reshape(6, 1, 1, 1, 1)
    base = jnp.clip(base * spread, -6.0, 6.0)
    return base.astype(jnp.bfloat16)


def shard_levels(own_key, dims, pieces, least, largest):
    def one(axis_at, shards_of):
        heights = jax.random.uniform(jax.random.fold_in(jax.random.fold_in(own_key, 6), axis_at), (shards_of,), jnp.float32, least / len(pieces), largest / len(pieces))
        return jnp.repeat(jnp.exp(heights), dims[axis_at] // shards_of).reshape((-1,) + (1,) * (len(dims) - axis_at - 1))

    loudness = one(*pieces[0])
    for cut in pieces[1:]:
        loudness = loudness * one(*cut)
    return loudness


def length_profile(amount, total, reach, lean):
    portions = [(1 << 20) // math.isqrt(grade ** lean) + 1 for grade in range(2, amount + 1)]
    surplus, given = total - reach - (amount - 1), [1] * (amount - 1)
    while surplus > 0:
        movable = [i for i in range(amount - 1) if given[i] < reach]
        whole, remaining = sum([portions[i] for i in movable]), surplus
        for i in movable:
            extra = min(reach - given[i], max(1, remaining * portions[i] // whole), surplus)
            given[i] = given[i] + extra
            surplus = surplus - extra
    return np.array([reach] + given)


def ragged_sizes(own_key, amount, total, reach, skew):
    if amount == 2:
        one = jax.random.randint(own_key, (), max(1, total - reach), min(reach, total - 1) + 1)
        return jnp.stack([one, total - one])
    lengths = jnp.asarray(length_profile(amount, total, reach, skew), jnp.int32)
    twos = (amount - 1) // 2
    source_of, sink = lengths[1:1 + 2 * twos:2], lengths[2:2 + 2 * twos:2]
    slack = jnp.minimum(source_of - 1, reach - sink)
    shifted = jax.random.randint(jax.random.fold_in(own_key, 1), (twos,), 0, 1 << 20) % (slack + 1)
    lengths = lengths.at[1:1 + 2 * twos:2].set(source_of - shifted).at[2:2 + 2 * twos:2].set(sink + shifted)
    return lengths[jax.random.permutation(jax.random.fold_in(own_key, 2), amount)]


def gaussian(key, shape, scale, limit, shards=(), kind=jnp.bfloat16):
    gain = shard_levels(key, shape, shards, -0.22, 0.18) if shards else 1.0
    values = jax.random.normal(key, shape, jnp.float32) * scale * gain
    return jnp.minimum(jnp.maximum(values, -limit), limit).astype(kind)


def setup_inputs(seed: int = 0) -> dict:
    splits = jax.random.split(jax.random.key(seed), 7)
    return {
        "projected": draw_projected(jax.random.fold_in(splits[6], 71), 0),
        "codes": gaussian(splits[1], (CLIPS, F, A), 1.0, 6.0, ((0, 4),), jnp.float32),
        "action_weight": gaussian(splits[2], (A, D), A ** -0.5, 1.0, ((1, 2),), jnp.float32),
        "clip_ids": jax.random.permutation(splits[3], CLIPS).astype(jnp.int32),
        "frame_map": jax.random.permutation(splits[4], F).astype(jnp.int32),
        "segments": jax.vmap(lambda own: jnp.searchsorted(jnp.cumsum(ragged_sizes(own, 3, F, 8, 0)), jnp.arange(F), side="right"))(jax.random.split(splits[5], CLIPS)).reshape((CLIPS, F)).astype(jnp.int32),
    }


def masked_softmax(spatial_scores, allowed):
    peak = jnp.max(jnp.where(allowed, spatial_scores, -1e30), axis=-1, keepdims=True)
    weights = jnp.where(allowed, jnp.exp(spatial_scores - peak), 0.0)
    return (weights / jnp.sum(weights, axis=-1, keepdims=True)).astype(jnp.bfloat16)


def reference(projected, codes, action_weight, clip_ids, frame_map, segments):
    heads = D // E
    reshaped_rows = projected.reshape(6, CLIPS, F, P_SIZE, heads, E)
    score_scale = 1.0 / (E ** 0.5)
    head_patches = lax.Precision.HIGHEST
    select = (clip_ids[:, None] == jnp.arange(CLIPS, dtype=jnp.int32)[None, :]).astype(jnp.float32)
    by_clip = jnp.einsum('ic,ifa->cfa', select, codes, precision=head_patches)
    action = jnp.einsum('cfa,ad->cfd', by_clip, action_weight, precision=head_patches)
    action_slot = action[:, frame_map]
    values = (reshaped_rows[5].astype(jnp.float32) + action_slot.reshape(CLIPS, F, 1, heads, E)).astype(jnp.bfloat16)
    seg_slot = segments[:, frame_map]
    allowed = (frame_map[None, :] <= frame_map[:, None])[None] & (seg_slot[:, None, :] == seg_slot[:, :, None])

    def per_clip(token_index):
        spatial_query = reshaped_rows[0, token_index].astype(jnp.float32)
        spatial_key = reshaped_rows[1, token_index].astype(jnp.float32)
        svalue = reshaped_rows[2, token_index].astype(jnp.float32)
        spatial_scores = jnp.einsum('bjvo,bcvo->bvjc', spatial_query, spatial_key, precision=head_patches) * score_scale
        probs = masked_softmax(spatial_scores, jnp.ones(spatial_scores.shape, bool))
        spatial = jnp.einsum('fhpq,fqhe->fphe', probs.astype(jnp.float32), svalue, precision=head_patches).astype(jnp.bfloat16)
        tquery = reshaped_rows[3, token_index].astype(jnp.float32)
        tkey = reshaped_rows[4, token_index].astype(jnp.float32)
        tvalue = values[token_index].astype(jnp.float32)
        tscores = jnp.einsum('sphe,tphe->phst', tquery, tkey, precision=head_patches) * score_scale
        tprobs = masked_softmax(tscores, allowed[token_index][None, None])
        temporal = jnp.einsum('phst,tphe->sphe', tprobs.astype(jnp.float32), tvalue, precision=head_patches).astype(jnp.bfloat16)
        return (spatial.astype(jnp.float32) + temporal.astype(jnp.float32)).astype(jnp.bfloat16)

    mixed = lax.map(per_clip, jnp.arange(CLIPS, dtype=jnp.int32))
    return mixed.reshape(CLIPS, F, P_SIZE, D)
```

```python
import functools

import jax
import jax.numpy as jnp
from jax import lax
from jax.experimental import pallas as pl
from jax.experimental.pallas import tpu as pltpu
from jax.sharding import PartitionSpec as P

E = 128
GROUP = 16
CHUNKS = 5
HIGHEST = lax.Precision.HIGHEST
VMEM = 48 * 1024 * 1024


def params():
    return pltpu.CompilerParams(vmem_limit_bytes=VMEM)


def spatial_kernel(q_ref, k_ref, v_ref, o_ref):
    heads = q_ref.shape[-1] // E
    for h in range(heads):
        cols = slice(h * E, (h + 1) * E)
        q, k, v = q_ref[0, 0, 0, :, cols], k_ref[0, 0, 0, :, cols], v_ref[0, 0, 0, :, cols]
        s = lax.dot_general(q, k, (((1,), (1,)), ((), ())), preferred_element_type=jnp.float32)
        s = s * (1.0 / E**0.5)
        w = jnp.exp(s - jnp.max(s, axis=-1, keepdims=True))
        p = (w * (1.0 / jnp.sum(w, axis=-1, keepdims=True))).astype(jnp.bfloat16)
        o = jnp.dot(p, v, preferred_element_type=jnp.float32)
        o_ref[0, 0, :, cols] = o.astype(jnp.bfloat16)


def spatial_attention(projected, step):
    _, clips, frames, patches, width = projected.shape
    spec = lambda which: pl.BlockSpec(
        (1, 1, 1, patches, step), lambda c, f, j: (which, c, f, 0, j)
    )
    return pl.pallas_call(
        spatial_kernel,
        grid=(clips, frames, width // step),
        in_specs=[spec(0), spec(1), spec(2)],
        out_specs=pl.BlockSpec((1, 1, patches, step), lambda c, f, j: (c, f, 0, j)),
        out_shape=jax.ShapeDtypeStruct((clips, frames, patches, width), jnp.bfloat16),
        compiler_params=params(),
        cost_estimate=pl.CostEstimate(
            flops=4 * clips * frames * patches * patches * width,
            bytes_accessed=8 * clips * frames * patches * width,
            transcendentals=clips * frames * patches * patches * (width // E),
        ),
        name="spatial",
    )(projected, projected, projected)


def pack_kernel(n, me_ref, *refs):
    for x, y in zip(refs[: n - 1], refs[n - 1 :]):
        y[...] = x[...]


def pack(projected, me, n, shifts, chunk, cols):
    _, clips, frames, patches, _ = projected.shape
    rows = patches // n
    block = (1, 1, frames, rows, cols)

    def spec(d):
        return pl.BlockSpec(
            block, lambda a, c, me_ref: (a + 3, c, 0, lax.rem(me_ref[0] + d, n), chunk)
        )

    shape = (3, clips, frames, rows, cols)
    return pl.pallas_call(
        functools.partial(pack_kernel, n),
        grid_spec=pltpu.PrefetchScalarGridSpec(
            num_scalar_prefetch=1,
            grid=(3, clips),
            in_specs=[spec(d) for d in shifts],
            out_specs=[pl.BlockSpec(block, lambda a, c, me_ref: (a, c, 0, 0, 0)) for _ in shifts],
        ),
        out_shape=[jax.ShapeDtypeStruct(shape, jnp.bfloat16) for _ in shifts],
        compiler_params=params(),
        cost_estimate=pl.CostEstimate(
            flops=0,
            bytes_accessed=12 * (n - 1) * clips * frames * rows * cols,
            transcendentals=0,
        ),
        name="pack",
    )(me, *([projected] * (n - 1)))


def temporal_kernel(n, me_ref, bias_ref, action_ref, *refs):
    ins, outs = refs[:n], refs[n:]
    frames, _, cols = ins[0].shape[2:]
    slots = n * frames
    bias = bias_ref[0]
    for h in range(cols // E):
        cut = slice(h * E, (h + 1) * E)

        def slots_of(which):
            return jnp.concatenate([x[which, 0, :, :, cut] for x in ins], axis=0)

        q = slots_of(0).reshape(slots * GROUP, E)
        k = slots_of(1).reshape(slots * GROUP, E)
        action = action_ref[0, :, cut].reshape(slots, 1, E)
        v = (slots_of(2).astype(jnp.float32) + action).astype(jnp.bfloat16)
        v = v.reshape(slots * GROUP, E)
        s = lax.dot_general(q, k, (((1,), (1,)), ((), ())), preferred_element_type=jnp.float32)
        s = s * (1.0 / E**0.5) + bias
        w = jnp.exp(s - jnp.max(s, axis=-1, keepdims=True))
        p = (w * (1.0 / jnp.sum(w, axis=-1, keepdims=True))).astype(jnp.bfloat16)
        o = jnp.dot(p, v, preferred_element_type=jnp.float32).astype(jnp.bfloat16)
        o = o.reshape(n, frames, GROUP, E)
        for i in range(n):
            outs[i][0, :, :, cut] = o[i]


def temporal_attention(projected, arrived, bias, action, me, n, chunk, cols):
    _, clips, frames, patches, _ = projected.shape
    rows = patches // n
    groups = rows // GROUP
    slots = n * frames
    block = (3, 1, frames, GROUP, cols)
    own = pl.BlockSpec(block, lambda c, g, me_ref: (1, c, 0, me_ref[0] * groups + g, chunk))
    other = pl.BlockSpec(block, lambda c, g, me_ref: (0, c, 0, g, 0))
    return pl.pallas_call(
        functools.partial(temporal_kernel, n),
        grid_spec=pltpu.PrefetchScalarGridSpec(
            num_scalar_prefetch=1,
            grid=(clips, groups),
            in_specs=[
                pl.BlockSpec((1, slots * GROUP, slots * GROUP), lambda c, g, me_ref: (c, 0, 0)),
                pl.BlockSpec((1, slots, cols), lambda c, g, me_ref: (c, 0, chunk)),
                own,
            ]
            + [other] * (n - 1),
            out_specs=[
                pl.BlockSpec((1, frames, GROUP, cols), lambda c, g, me_ref: (c, 0, g, 0))
            ]
            * n,
        ),
        out_shape=[jax.ShapeDtypeStruct((clips, frames, rows, cols), jnp.bfloat16)] * n,
        compiler_params=params(),
        cost_estimate=pl.CostEstimate(
            flops=4 * clips * groups * (slots * GROUP) ** 2 * cols,
            bytes_accessed=8 * clips * slots * rows * cols,
            transcendentals=clips * groups * (slots * GROUP) ** 2 * (cols // E),
        ),
        name="temporal",
    )(me, bias, action, projected, *arrived)


def combine_kernel(n, me_ref, spatial_ref, *refs):
    parts, out_ref = refs[:n], refs[n]
    rows = parts[0].shape[2]
    for d in range(n):
        at = pl.ds(pl.multiple_of(lax.rem(me_ref[0] + d, n) * rows, rows), rows)
        total = spatial_ref[0, :, at, :].astype(jnp.float32) + parts[d][0].astype(jnp.float32)
        out_ref[0, :, at, :] = total.astype(jnp.bfloat16)


def combine(mixed, parts, me, n, chunk, cols):
    clips, frames, patches, width = mixed.shape
    rows = patches // n
    whole = pl.BlockSpec((1, frames, patches, cols), lambda c, me_ref: (c, 0, 0, chunk))
    part = pl.BlockSpec((1, frames, rows, cols), lambda c, me_ref: (c, 0, 0, 0))
    return pl.pallas_call(
        functools.partial(combine_kernel, n),
        grid_spec=pltpu.PrefetchScalarGridSpec(
            num_scalar_prefetch=1,
            grid=(clips,),
            in_specs=[whole] + [part] * n,
            out_specs=whole,
        ),
        out_shape=jax.ShapeDtypeStruct(mixed.shape, mixed.dtype),
        input_output_aliases={1: 0},
        compiler_params=params(),
        cost_estimate=pl.CostEstimate(
            flops=clips * frames * patches * cols,
            bytes_accessed=6 * clips * frames * patches * cols,
            transcendentals=0,
        ),
        name="combine",
    )(me, mixed, *parts)


def local(n, projected, codes, action_weight, clip_ids, frame_map, segments):
    _, clips, frames, patches, width = projected.shape
    slots = frame_map.shape[0]
    heads = width // E
    chunks = max(c for c in range(1, CHUNKS + 1) if heads % c == 0)
    cols = width // chunks
    me_scalar = lax.axis_index("frame")
    me = me_scalar.astype(jnp.int32)[None]
    far_first = sorted(range(1, n), key=lambda d: abs(d - n // 2))

    def send(x, d):
        return lax.ppermute(x, "frame", [(i, (i + d) % n) for i in range(n)])

    arrived = []
    for j in range(chunks):
        packed = pack(projected, me, n, far_first, j, cols)
        got = {d: send(x, d) for d, x in zip(far_first, packed)}
        arrived.append([got[d] for d in range(1, n)])

    source = lax.rem(me_scalar - jnp.arange(n) + n, n)
    order = (source[:, None] * frames + jnp.arange(frames)[None, :]).reshape(-1)
    time_of = jnp.sum(
        jnp.where(order[:, None] == jnp.arange(slots)[None, :], frame_map[None, :], 0), axis=-1
    )
    at_time = time_of[:, None] == jnp.arange(slots, dtype=jnp.int32)[None, :]
    seg_slot = jnp.sum(jnp.where(at_time[None], segments[:, None, :], 0), axis=-1)
    allowed = (time_of[None, :] <= time_of[:, None])[None] & (
        seg_slot[:, None, :] == seg_slot[:, :, None]
    )
    row = jnp.arange(slots * GROUP)
    same_patch = (row[:, None] % GROUP) == (row[None, :] % GROUP)
    wide = jnp.repeat(jnp.repeat(allowed, GROUP, axis=1), GROUP, axis=2)
    bias = jnp.where(wide & same_patch[None], 0.0, -1e30).astype(jnp.float32)

    all_codes = lax.all_gather(codes, "dp", axis=0, tiled=True)
    owned = lax.axis_index("dp") * clips + jnp.arange(clips, dtype=jnp.int32)
    select = (clip_ids[:, None] == owned[None, :]).astype(jnp.float32)
    by_clip = jnp.einsum("ic,ifa->cfa", select, all_codes, precision=HIGHEST)
    codes_slot = jnp.einsum(
        "st,cta->csa", at_time.astype(jnp.float32), by_clip, precision=HIGHEST
    )
    action = jnp.einsum("csa,ad->csd", codes_slot, action_weight, precision=HIGHEST)

    mixed = spatial_attention(projected, cols)
    for j in range(chunks):
        done = temporal_attention(projected, arrived[j], bias, action, me, n, j, cols)
        back = {d: send(done[d], -d) for d in far_first}
        mixed = combine(mixed, [done[0]] + [back[d] for d in range(1, n)], me, n, j, cols)
    return mixed


def solution(mesh):
    return jax.shard_map(
        functools.partial(local, mesh.shape["frame"]),
        mesh=mesh,
        in_specs=(
            P(None, "dp", "frame", None, "mp"),
            P("dp", None, None),
            P(None, "mp"),
            P(),
            P(),
            P("dp", None),
        ),
        out_specs=P("dp", "frame", None, "mp"),
        check_vma=False,
    )
```

```python
import functools

import jax
import jax.numpy as jnp
from jax import lax
from jax.experimental import pallas as pl
from jax.experimental.pallas import tpu as pltpu
from jax.sharding import PartitionSpec as P

E = 128
GROUP = 16
CHUNKS = 5
AHEAD = 2
HIGHEST = lax.Precision.HIGHEST
VMEM = 48 * 1024 * 1024


def params():
    return pltpu.CompilerParams(vmem_limit_bytes=VMEM)


def spatial_kernel(q_ref, k_ref, v_ref, o_ref):
    heads = q_ref.shape[-1] // E
    for h in range(heads):
        cols = slice(h * E, (h + 1) * E)
        q, k, v = q_ref[0, 0, 0, :, cols], k_ref[0, 0, 0, :, cols], v_ref[0, 0, 0, :, cols]
        s = lax.dot_general(q, k, (((1,), (1,)), ((), ())), preferred_element_type=jnp.float32)
        s = s * (1.0 / E**0.5)
        w = jnp.exp(s - jnp.max(s, axis=-1, keepdims=True))
        p = (w * (1.0 / jnp.sum(w, axis=-1, keepdims=True))).astype(jnp.bfloat16)
        o = jnp.dot(p, v, preferred_element_type=jnp.float32)
        o_ref[0, 0, :, cols] = o.astype(jnp.bfloat16)


def spatial_attention(projected, chunk, cols):
    _, clips, frames, patches, _ = projected.shape
    spec = lambda which: pl.BlockSpec(
        (1, 1, 1, patches, cols), lambda c, f: (which, c, f, 0, chunk)
    )
    return pl.pallas_call(
        spatial_kernel,
        grid=(clips, frames),
        in_specs=[spec(0), spec(1), spec(2)],
        out_specs=pl.BlockSpec((1, 1, patches, cols), lambda c, f: (c, f, 0, 0)),
        out_shape=jax.ShapeDtypeStruct((clips, frames, patches, cols), jnp.bfloat16),
        compiler_params=params(),
        cost_estimate=pl.CostEstimate(
            flops=4 * clips * frames * patches * patches * cols,
            bytes_accessed=8 * clips * frames * patches * cols,
            transcendentals=clips * frames * patches * patches * (cols // E),
        ),
        name="spatial",
    )(projected, projected, projected)


def pack_kernel(n, me_ref, *refs):
    for x, y in zip(refs[: n - 1], refs[n - 1 :]):
        y[...] = x[...]


def pack(projected, me, n, shifts, chunk, cols):
    _, clips, frames, patches, _ = projected.shape
    rows = patches // n
    block = (1, 1, frames, rows, cols)

    def spec(d):
        return pl.BlockSpec(
            block, lambda a, c, me_ref: (a + 3, c, 0, lax.rem(me_ref[0] + d, n), chunk)
        )

    shape = (3, clips, frames, rows, cols)
    return pl.pallas_call(
        functools.partial(pack_kernel, n),
        grid_spec=pltpu.PrefetchScalarGridSpec(
            num_scalar_prefetch=1,
            grid=(3, clips),
            in_specs=[spec(d) for d in shifts],
            out_specs=[pl.BlockSpec(block, lambda a, c, me_ref: (a, c, 0, 0, 0)) for _ in shifts],
        ),
        out_shape=[jax.ShapeDtypeStruct(shape, jnp.bfloat16) for _ in shifts],
        compiler_params=params(),
        cost_estimate=pl.CostEstimate(
            flops=0,
            bytes_accessed=12 * (n - 1) * clips * frames * rows * cols,
            transcendentals=0,
        ),
        name="pack",
    )(me, *([projected] * (n - 1)))


def temporal_kernel(n, me_ref, bias_ref, action_ref, *refs):
    ins, outs = refs[:n], refs[n:]
    frames, _, cols = ins[0].shape[2:]
    slots = n * frames
    bias = bias_ref[0]
    for h in range(cols // E):
        cut = slice(h * E, (h + 1) * E)

        def slots_of(which):
            return jnp.concatenate([x[which, 0, :, :, cut] for x in ins], axis=0)

        q = slots_of(0).reshape(slots * GROUP, E)
        k = slots_of(1).reshape(slots * GROUP, E)
        action = action_ref[0, :, cut].reshape(slots, 1, E)
        v = (slots_of(2).astype(jnp.float32) + action).astype(jnp.bfloat16)
        v = v.reshape(slots * GROUP, E)
        s = lax.dot_general(q, k, (((1,), (1,)), ((), ())), preferred_element_type=jnp.float32)
        s = s * (1.0 / E**0.5) + bias
        w = jnp.exp(s - jnp.max(s, axis=-1, keepdims=True))
        p = (w * (1.0 / jnp.sum(w, axis=-1, keepdims=True))).astype(jnp.bfloat16)
        o = jnp.dot(p, v, preferred_element_type=jnp.float32).astype(jnp.bfloat16)
        o = o.reshape(n, frames, GROUP, E)
        for i in range(n):
            outs[i][0, :, :, cut] = o[i]


def temporal_attention(projected, arrived, bias, action, me, n, chunk, cols):
    _, clips, frames, patches, _ = projected.shape
    rows = patches // n
    groups = rows // GROUP
    slots = n * frames
    block = (3, 1, frames, GROUP, cols)
    own = pl.BlockSpec(block, lambda c, g, me_ref: (1, c, 0, me_ref[0] * groups + g, chunk))
    other = pl.BlockSpec(block, lambda c, g, me_ref: (0, c, 0, g, 0))
    return pl.pallas_call(
        functools.partial(temporal_kernel, n),
        grid_spec=pltpu.PrefetchScalarGridSpec(
            num_scalar_prefetch=1,
            grid=(clips, groups),
            in_specs=[
                pl.BlockSpec((1, slots * GROUP, slots * GROUP), lambda c, g, me_ref: (c, 0, 0)),
                pl.BlockSpec((1, slots, cols), lambda c, g, me_ref: (c, 0, chunk)),
                own,
            ]
            + [other] * (n - 1),
            out_specs=[
                pl.BlockSpec((1, frames, GROUP, cols), lambda c, g, me_ref: (c, 0, g, 0))
            ]
            * n,
        ),
        out_shape=[jax.ShapeDtypeStruct((clips, frames, rows, cols), jnp.bfloat16)] * n,
        compiler_params=params(),
        cost_estimate=pl.CostEstimate(
            flops=4 * clips * groups * (slots * GROUP) ** 2 * cols,
            bytes_accessed=8 * clips * slots * rows * cols,
            transcendentals=clips * groups * (slots * GROUP) ** 2 * (cols // E),
        ),
        name="temporal",
    )(me, bias, action, projected, *arrived)


def combine_kernel(n, me_ref, spatial_ref, *refs):
    parts, out_ref = refs[:n], refs[-1]
    rows = parts[0].shape[2]
    for d in range(n):
        at = pl.ds(pl.multiple_of(lax.rem(me_ref[0] + d, n) * rows, rows), rows)
        total = spatial_ref[0, :, at, :].astype(jnp.float32) + parts[d][0].astype(jnp.float32)
        out_ref[0, :, at, :] = total.astype(jnp.bfloat16)


def combine(mixed, spatial, parts, me, n, chunk, width):
    clips, frames, patches, cols = spatial.shape
    rows = patches // n
    part = pl.BlockSpec((1, frames, rows, cols), lambda c, me_ref: (c, 0, 0, 0))
    before = [] if mixed is None else [mixed]
    return pl.pallas_call(
        functools.partial(combine_kernel, n),
        grid_spec=pltpu.PrefetchScalarGridSpec(
            num_scalar_prefetch=1,
            grid=(clips,),
            in_specs=[pl.BlockSpec((1, frames, patches, cols), lambda c, me_ref: (c, 0, 0, 0))]
            + [part] * n
            + [pl.BlockSpec(memory_space=pl.ANY)] * len(before),
            out_specs=pl.BlockSpec((1, frames, patches, cols), lambda c, me_ref: (c, 0, 0, chunk)),
        ),
        out_shape=jax.ShapeDtypeStruct((clips, frames, patches, width), jnp.bfloat16),
        input_output_aliases={n + 2: 0} if before else {},
        compiler_params=params(),
        cost_estimate=pl.CostEstimate(
            flops=clips * frames * patches * cols,
            bytes_accessed=6 * clips * frames * patches * cols,
            transcendentals=0,
        ),
        name="combine",
    )(me, spatial, *parts, *before)


def after(x, *others):
    return lax.optimization_barrier((x, *others))[0]


def local(n, projected, codes, action_weight, clip_ids, frame_map, segments):
    _, clips, frames, patches, width = projected.shape
    slots = frame_map.shape[0]
    heads = width // E
    chunks = max(c for c in range(1, CHUNKS + 1) if heads % c == 0)
    cols = width // chunks
    me_scalar = lax.axis_index("frame")
    me = me_scalar.astype(jnp.int32)[None]
    far_first = sorted(range(1, n), key=lambda d: abs(d - n // 2))

    def send(x, d):
        return lax.ppermute(x, "frame", [(i, (i + d) % n) for i in range(n)])

    def forward(j, *others):
        packed = pack(projected, me, n, far_first, j, cols)
        if others:
            packed = lax.optimization_barrier((*packed, *others))[: n - 1]
        got = {d: send(x, d) for d, x in zip(far_first, packed)}
        return [got[d] for d in range(1, n)]

    arrived = [forward(j) for j in range(min(AHEAD, chunks))]

    source = lax.rem(me_scalar - jnp.arange(n) + n, n)
    order = (source[:, None] * frames + jnp.arange(frames)[None, :]).reshape(-1)
    time_of = jnp.sum(
        jnp.where(order[:, None] == jnp.arange(slots)[None, :], frame_map[None, :], 0), axis=-1
    )
    at_time = time_of[:, None] == jnp.arange(slots, dtype=jnp.int32)[None, :]
    seg_slot = jnp.sum(jnp.where(at_time[None], segments[:, None, :], 0), axis=-1)
    allowed = (time_of[None, :] <= time_of[:, None])[None] & (
        seg_slot[:, None, :] == seg_slot[:, :, None]
    )
    row = jnp.arange(slots * GROUP)
    same_patch = (row[:, None] % GROUP) == (row[None, :] % GROUP)
    wide = jnp.repeat(jnp.repeat(allowed, GROUP, axis=1), GROUP, axis=2)
    bias = jnp.where(wide & same_patch[None], 0.0, -1e30).astype(jnp.float32)

    all_codes = lax.all_gather(codes, "dp", axis=0, tiled=True)
    owned = lax.axis_index("dp") * clips + jnp.arange(clips, dtype=jnp.int32)
    select = (clip_ids[:, None] == owned[None, :]).astype(jnp.float32)
    by_clip = jnp.einsum("ic,ifa->cfa", select, all_codes, precision=HIGHEST)
    codes_slot = jnp.einsum(
        "st,cta->csa", at_time.astype(jnp.float32), by_clip, precision=HIGHEST
    )
    action = jnp.einsum("csa,ad->csd", codes_slot, action_weight, precision=HIGHEST)

    mixed = None
    for j in range(chunks):
        spatial = spatial_attention(projected, j, cols)
        done = temporal_attention(
            projected, arrived[j], bias, action, after(me, spatial), n, j, cols
        )
        back = {d: send(done[d], -d) for d in far_first}
        if j + AHEAD < chunks:
            arrived.append(forward(j + AHEAD, done[1]))
        parts = [done[0]] + [back[d] for d in range(1, n)]
        mixed = combine(mixed, spatial, parts, me, n, j, width)
    return mixed


def solution(mesh):
    return jax.shard_map(
        functools.partial(local, mesh.shape["frame"]),
        mesh=mesh,
        in_specs=(
            P(None, "dp", "frame", None, "mp"),
            P("dp", None, None),
            P(None, "mp"),
            P(),
            P(),
            P("dp", None),
        ),
        out_specs=P("dp", "frame", None, "mp"),
        check_vma=False,
    )
```

```python
import functools

import jax
import jax.numpy as jnp
from jax import lax
from jax.experimental import pallas as pl
from jax.experimental.pallas import tpu as pltpu
from jax.sharding import PartitionSpec as P

E = 128
GROUP = 16
CHUNKS = 5
AHEAD = 2
HIGHEST = lax.Precision.HIGHEST
VMEM = 48 * 1024 * 1024


def params():
    return pltpu.CompilerParams(vmem_limit_bytes=VMEM)


def spatial_kernel(q_ref, k_ref, v_ref, o_ref):
    heads = q_ref.shape[-1] // E
    for h in range(heads):
        cols = slice(h * E, (h + 1) * E)
        q, k, v = q_ref[0, 0, 0, :, cols], k_ref[0, 0, 0, :, cols], v_ref[0, 0, 0, :, cols]
        s = lax.dot_general(q, k, (((1,), (1,)), ((), ())), preferred_element_type=jnp.float32)
        s = s * (1.0 / E**0.5)
        w = jnp.exp(s - jnp.max(s, axis=-1, keepdims=True))
        p = (w * (1.0 / jnp.sum(w, axis=-1, keepdims=True))).astype(jnp.bfloat16)
        o = jnp.dot(p, v, preferred_element_type=jnp.float32)
        o_ref[0, 0, :, cols] = o.astype(jnp.bfloat16)


def spatial_attention(projected, chunk, cols):
    _, clips, frames, patches, _ = projected.shape
    spec = lambda which: pl.BlockSpec(
        (1, 1, 1, patches, cols), lambda c, f: (which, c, f, 0, chunk)
    )
    return pl.pallas_call(
        spatial_kernel,
        grid=(clips, frames),
        in_specs=[spec(0), spec(1), spec(2)],
        out_specs=pl.BlockSpec((1, 1, patches, cols), lambda c, f: (c, f, 0, 0)),
        out_shape=jax.ShapeDtypeStruct((clips, frames, patches, cols), jnp.bfloat16),
        compiler_params=params(),
        cost_estimate=pl.CostEstimate(
            flops=4 * clips * frames * patches * patches * cols,
            bytes_accessed=8 * clips * frames * patches * cols,
            transcendentals=clips * frames * patches * patches * (cols // E),
        ),
        name="spatial",
    )(projected, projected, projected)


def pack_kernel(me_ref, *refs):
    count = len(refs) // 2
    for x, y in zip(refs[:count], refs[count:]):
        y[...] = x[...]


def pack(projected, me, n, shifts, chunk, cols):
    _, clips, frames, patches, _ = projected.shape
    rows = patches // n
    block = (1, 1, frames, rows, cols)

    def spec(d):
        return pl.BlockSpec(
            block, lambda a, c, me_ref: (a + 3, c, 0, lax.rem(me_ref[0] + d, n), chunk)
        )

    shape = (3, clips, frames, rows, cols)
    return pl.pallas_call(
        pack_kernel,
        grid_spec=pltpu.PrefetchScalarGridSpec(
            num_scalar_prefetch=1,
            grid=(3, clips),
            in_specs=[spec(d) for d in shifts],
            out_specs=[pl.BlockSpec(block, lambda a, c, me_ref: (a, c, 0, 0, 0)) for _ in shifts],
        ),
        out_shape=[jax.ShapeDtypeStruct(shape, jnp.bfloat16) for _ in shifts],
        compiler_params=params(),
        cost_estimate=pl.CostEstimate(
            flops=0,
            bytes_accessed=12 * len(shifts) * clips * frames * rows * cols,
            transcendentals=0,
        ),
        name="pack",
    )(me, *([projected] * len(shifts)))


def temporal_kernel(n, me_ref, bias_ref, action_ref, *refs):
    ins, outs = refs[:n], refs[n:]
    frames, _, cols = ins[0].shape[2:]
    slots = n * frames
    bias = bias_ref[0]
    for h in range(cols // E):
        cut = slice(h * E, (h + 1) * E)

        def slots_of(which):
            return jnp.concatenate([x[which, 0, :, :, cut] for x in ins], axis=0)

        q = slots_of(0).reshape(slots * GROUP, E)
        k = slots_of(1).reshape(slots * GROUP, E)
        action = action_ref[0, :, cut].reshape(slots, 1, E)
        v = (slots_of(2).astype(jnp.float32) + action).astype(jnp.bfloat16)
        v = v.reshape(slots * GROUP, E)
        s = lax.dot_general(q, k, (((1,), (1,)), ((), ())), preferred_element_type=jnp.float32)
        s = s * (1.0 / E**0.5) + bias
        w = jnp.exp(s - jnp.max(s, axis=-1, keepdims=True))
        p = (w * (1.0 / jnp.sum(w, axis=-1, keepdims=True))).astype(jnp.bfloat16)
        o = jnp.dot(p, v, preferred_element_type=jnp.float32).astype(jnp.bfloat16)
        o = o.reshape(n, frames, GROUP, E)
        for i in range(n):
            outs[i][0, :, :, cut] = o[i]


def temporal_attention(projected, arrived, bias, action, me, n, chunk, cols):
    _, clips, frames, patches, _ = projected.shape
    rows = patches // n
    groups = rows // GROUP
    slots = n * frames
    block = (3, 1, frames, GROUP, cols)
    own = pl.BlockSpec(block, lambda c, g, me_ref: (1, c, 0, me_ref[0] * groups + g, chunk))
    other = pl.BlockSpec(block, lambda c, g, me_ref: (0, c, 0, g, 0))
    return pl.pallas_call(
        functools.partial(temporal_kernel, n),
        grid_spec=pltpu.PrefetchScalarGridSpec(
            num_scalar_prefetch=1,
            grid=(clips, groups),
            in_specs=[
                pl.BlockSpec((1, slots * GROUP, slots * GROUP), lambda c, g, me_ref: (c, 0, 0)),
                pl.BlockSpec((1, slots, cols), lambda c, g, me_ref: (c, 0, chunk)),
                own,
            ]
            + [other] * (n - 1),
            out_specs=[
                pl.BlockSpec((1, frames, GROUP, cols), lambda c, g, me_ref: (c, 0, g, 0))
            ]
            * n,
        ),
        out_shape=[jax.ShapeDtypeStruct((clips, frames, rows, cols), jnp.bfloat16)] * n,
        compiler_params=params(),
        cost_estimate=pl.CostEstimate(
            flops=4 * clips * groups * (slots * GROUP) ** 2 * cols,
            bytes_accessed=8 * clips * slots * rows * cols,
            transcendentals=clips * groups * (slots * GROUP) ** 2 * (cols // E),
        ),
        name="temporal",
    )(me, bias, action, projected, *arrived)


def combine_kernel(n, me_ref, spatial_ref, *refs):
    parts, out_ref = refs[:n], refs[-1]
    rows = parts[0].shape[2]
    for d in range(n):
        at = pl.ds(pl.multiple_of(lax.rem(me_ref[0] + d, n) * rows, rows), rows)
        total = spatial_ref[0, :, at, :].astype(jnp.float32) + parts[d][0].astype(jnp.float32)
        out_ref[0, :, at, :] = total.astype(jnp.bfloat16)


def combine(mixed, spatial, parts, me, n, chunk, width):
    clips, frames, patches, cols = spatial.shape
    rows = patches // n
    part = pl.BlockSpec((1, frames, rows, cols), lambda c, me_ref: (c, 0, 0, 0))
    before = [] if mixed is None else [mixed]
    return pl.pallas_call(
        functools.partial(combine_kernel, n),
        grid_spec=pltpu.PrefetchScalarGridSpec(
            num_scalar_prefetch=1,
            grid=(clips,),
            in_specs=[pl.BlockSpec((1, frames, patches, cols), lambda c, me_ref: (c, 0, 0, 0))]
            + [part] * n
            + [pl.BlockSpec(memory_space=pl.ANY)] * len(before),
            out_specs=pl.BlockSpec((1, frames, patches, cols), lambda c, me_ref: (c, 0, 0, chunk)),
        ),
        out_shape=jax.ShapeDtypeStruct((clips, frames, patches, width), jnp.bfloat16),
        input_output_aliases={n + 2: 0} if before else {},
        compiler_params=params(),
        cost_estimate=pl.CostEstimate(
            flops=clips * frames * patches * cols,
            bytes_accessed=6 * clips * frames * patches * cols,
            transcendentals=0,
        ),
        name="combine",
    )(me, spatial, *parts, *before)


def after(x, *others):
    return lax.optimization_barrier((x, *others))[0]


def chunk_sizes(heads):
    least, most = max(1, heads // (2 * CHUNKS)), max(1, heads // CHUNKS)
    sizes, at = [], 0
    while at < heads:
        limit = max(least, min(most, (heads - at) // 2)) if at >= most else least
        limit = min(limit, heads - at)
        sizes.append(max(c for c in range(1, limit + 1) if at % c == 0))
        at += sizes[-1]
    return sizes


def local(n, projected, codes, action_weight, clip_ids, frame_map, segments):
    _, clips, frames, patches, width = projected.shape
    slots = frame_map.shape[0]
    heads = width // E
    sizes = chunk_sizes(heads)
    chunks = len(sizes)
    starts = [sum(sizes[:j]) for j in range(chunks)]
    me_scalar = lax.axis_index("frame")
    me = me_scalar.astype(jnp.int32)[None]
    far_first = sorted(range(1, n), key=lambda d: abs(d - n // 2))

    def send(x, d):
        return lax.ppermute(x, "frame", [(i, (i + d) % n) for i in range(n)])

    def forward(j, *others):
        cols = sizes[j] * E
        at = starts[j] // sizes[j]
        if j == 0:
            packed = [pack(projected, me, n, [d], at, cols)[0] for d in far_first]
        else:
            packed = pack(projected, me, n, far_first, at, cols)
        if others:
            packed = lax.optimization_barrier((*packed, *others))[: n - 1]
        got = {d: send(x, d) for d, x in zip(far_first, packed)}
        return [got[d] for d in range(1, n)]

    arrived = [forward(j) for j in range(min(AHEAD, chunks))]

    source = lax.rem(me_scalar - jnp.arange(n) + n, n)
    order = (source[:, None] * frames + jnp.arange(frames)[None, :]).reshape(-1)
    time_of = jnp.sum(
        jnp.where(order[:, None] == jnp.arange(slots)[None, :], frame_map[None, :], 0), axis=-1
    )
    at_time = time_of[:, None] == jnp.arange(slots, dtype=jnp.int32)[None, :]
    seg_slot = jnp.sum(jnp.where(at_time[None], segments[:, None, :], 0), axis=-1)
    allowed = (time_of[None, :] <= time_of[:, None])[None] & (
        seg_slot[:, None, :] == seg_slot[:, :, None]
    )
    row = jnp.arange(slots * GROUP)
    same_patch = (row[:, None] % GROUP) == (row[None, :] % GROUP)
    wide = jnp.repeat(jnp.repeat(allowed, GROUP, axis=1), GROUP, axis=2)
    bias = jnp.where(wide & same_patch[None], 0.0, -1e30).astype(jnp.float32)

    all_codes = lax.all_gather(codes, "dp", axis=0, tiled=True)
    owned = lax.axis_index("dp") * clips + jnp.arange(clips, dtype=jnp.int32)
    select = (clip_ids[:, None] == owned[None, :]).astype(jnp.float32)
    by_clip = jnp.einsum("ic,ifa->cfa", select, all_codes, precision=HIGHEST)
    codes_slot = jnp.einsum(
        "st,cta->csa", at_time.astype(jnp.float32), by_clip, precision=HIGHEST
    )
    action = jnp.einsum("csa,ad->csd", codes_slot, action_weight, precision=HIGHEST)

    spatial = []
    mixed = None
    for j in range(chunks):
        cols, at = sizes[j] * E, starts[j] // sizes[j]
        while len(spatial) < min(j + 2, chunks):
            i = len(spatial)
            spatial.append(spatial_attention(projected, starts[i] // sizes[i], sizes[i] * E))
        done = temporal_attention(
            projected, arrived[j], bias, action, after(me, *spatial), n, at, cols
        )
        back = {d: send(done[d], -d) for d in far_first}
        if j + AHEAD < chunks:
            arrived.append(forward(j + AHEAD, done[1]))
        parts = [done[0]] + [back[d] for d in range(1, n)]
        mixed = combine(mixed, spatial[j], parts, me, n, at, width)
    return mixed


def solution(mesh):
    return jax.shard_map(
        functools.partial(local, mesh.shape["frame"]),
        mesh=mesh,
        in_specs=(
            P(None, "dp", "frame", None, "mp"),
            P("dp", None, None),
            P(None, "mp"),
            P(),
            P(),
            P("dp", None),
        ),
        out_specs=P("dp", "frame", None, "mp"),
        check_vma=False,
    )
```

```python
import functools

import jax
import jax.numpy as jnp
from jax import lax
from jax.experimental import pallas as pl
from jax.experimental.pallas import tpu as pltpu
from jax.sharding import PartitionSpec as P

E = 128
GROUP = 16
CHUNKS = 5
AHEAD = 2
HIGHEST = lax.Precision.HIGHEST
VMEM = 48 * 1024 * 1024


def params():
    return pltpu.CompilerParams(vmem_limit_bytes=VMEM)


def spatial_kernel(q_ref, k_ref, v_ref, o_ref):
    heads = q_ref.shape[-1] // E
    for h in range(heads):
        cols = slice(h * E, (h + 1) * E)
        q, k, v = q_ref[0, 0, 0, :, cols], k_ref[0, 0, 0, :, cols], v_ref[0, 0, 0, :, cols]
        s = lax.dot_general(q, k, (((1,), (1,)), ((), ())), preferred_element_type=jnp.float32)
        s = s * (1.0 / E**0.5)
        w = jnp.exp(s - jnp.max(s, axis=-1, keepdims=True))
        p = (w * (1.0 / jnp.sum(w, axis=-1, keepdims=True))).astype(jnp.bfloat16)
        o = jnp.dot(p, v, preferred_element_type=jnp.float32)
        o_ref[0, 0, :, cols] = o.astype(jnp.bfloat16)


def spatial_attention(projected, chunk, cols):
    _, clips, frames, patches, _ = projected.shape
    spec = lambda which: pl.BlockSpec(
        (1, 1, 1, patches, cols), lambda c, f: (which, c, f, 0, chunk)
    )
    return pl.pallas_call(
        spatial_kernel,
        grid=(clips, frames),
        in_specs=[spec(0), spec(1), spec(2)],
        out_specs=pl.BlockSpec((1, 1, patches, cols), lambda c, f: (c, f, 0, 0)),
        out_shape=jax.ShapeDtypeStruct((clips, frames, patches, cols), jnp.bfloat16),
        compiler_params=params(),
        cost_estimate=pl.CostEstimate(
            flops=4 * clips * frames * patches * patches * cols,
            bytes_accessed=8 * clips * frames * patches * cols,
            transcendentals=clips * frames * patches * patches * (cols // E),
        ),
        name="spatial",
    )(projected, projected, projected)


def copy_units(x_ref, which, y_ref, at):
    heads = x_ref.shape[-1] // E
    for h in range(heads):
        y_ref[at + h, 0] = x_ref[which, 0, :, :, h * E : (h + 1) * E]


def pack_kernel(me_ref, *refs):
    count = len(refs) // 2
    for x, y in zip(refs[:count], refs[count:]):
        copy_units(x, 0, y, 0)


def pack(projected, me, n, shifts, chunk, heads):
    _, clips, frames, patches, _ = projected.shape
    rows = patches // n

    def spec(d):
        return pl.BlockSpec(
            (1, 1, frames, rows, heads * E),
            lambda a, c, me_ref: (a + 3, c, 0, lax.rem(me_ref[0] + d, n), chunk),
        )

    out_spec = pl.BlockSpec((heads, 1, frames, rows, E), lambda a, c, me_ref: (a, c, 0, 0, 0))
    shape = jax.ShapeDtypeStruct((3 * heads, clips, frames, rows, E), jnp.bfloat16)
    return pl.pallas_call(
        pack_kernel,
        grid_spec=pltpu.PrefetchScalarGridSpec(
            num_scalar_prefetch=1,
            grid=(3, clips),
            in_specs=[spec(d) for d in shifts],
            out_specs=[out_spec] * len(shifts),
        ),
        out_shape=[shape] * len(shifts),
        compiler_params=params(),
        cost_estimate=pl.CostEstimate(
            flops=0,
            bytes_accessed=12 * len(shifts) * clips * frames * rows * heads * E,
            transcendentals=0,
        ),
        name="pack",
    )(me, *([projected] * len(shifts)))


def temporal_kernel(n, heads, skip, later, me_ref, bias_ref, action_ref, own_ref, *refs):
    arrived, refs = refs[: n - 1], refs[n - 1 :]
    ahead, refs = (refs[: n - 1], refs[n - 1 :]) if later else ((), refs)
    own_out, outs = refs[0], refs[1:]
    frames = own_ref.shape[2]
    slots = n * frames
    bias = bias_ref[0]
    for h in range(heads):
        cut = slice(h * E, (h + 1) * E)

        def slots_of(which):
            unit = skip + which * heads + h
            parts = [own_ref[which, 0, :, :, cut]] + [x[unit, 0] for x in arrived]
            return jnp.concatenate(parts, axis=0)

        q = slots_of(0).reshape(slots * GROUP, E)
        k = slots_of(1).reshape(slots * GROUP, E)
        action = action_ref[0, :, cut].reshape(slots, 1, E)
        v = (slots_of(2).astype(jnp.float32) + action).astype(jnp.bfloat16)
        v = v.reshape(slots * GROUP, E)
        s = lax.dot_general(q, k, (((1,), (1,)), ((), ())), preferred_element_type=jnp.float32)
        s = s * (1.0 / E**0.5) + bias
        w = jnp.exp(s - jnp.max(s, axis=-1, keepdims=True))
        p = (w * (1.0 / jnp.sum(w, axis=-1, keepdims=True))).astype(jnp.bfloat16)
        o = jnp.dot(p, v, preferred_element_type=jnp.float32).astype(jnp.bfloat16)
        o = o.reshape(n, frames, GROUP, E)
        own_out[h, 0] = o[0]
        for e in range(1, n):
            outs[e - 1][h, 0] = o[n - e]
    for e in range(1, n if later else 1):
        for which in range(3):
            copy_units(ahead[e - 1], which, outs[e - 1], heads + which * later)


def temporal_attention(
    projected, arrived, skip, bias, action, me, n, chunk, heads, later_chunk=0, later=0
):
    _, clips, frames, patches, _ = projected.shape
    rows = patches // n
    groups = rows // GROUP
    slots = n * frames

    def rows_of(device, at, count):
        return pl.BlockSpec(
            (3, 1, frames, GROUP, count * E),
            lambda c, g, me_ref: (1, c, 0, lax.rem(me_ref[0] + device, n) * groups + g, at),
        )

    def units(count):
        return pl.BlockSpec((count, 1, frames, GROUP, E), lambda c, g, me_ref: (0, c, 0, g, 0))

    out = lambda count: jax.ShapeDtypeStruct((count, clips, frames, rows, E), jnp.bfloat16)
    sent = heads + 3 * later
    ahead = range(1, n) if later else ()
    return pl.pallas_call(
        functools.partial(temporal_kernel, n, heads, skip, later),
        grid_spec=pltpu.PrefetchScalarGridSpec(
            num_scalar_prefetch=1,
            grid=(clips, groups),
            in_specs=[
                pl.BlockSpec((1, slots * GROUP, slots * GROUP), lambda c, g, me_ref: (c, 0, 0)),
                pl.BlockSpec((1, slots, heads * E), lambda c, g, me_ref: (c, 0, chunk)),
                rows_of(0, chunk, heads),
            ]
            + [units(skip + 3 * heads)] * (n - 1)
            + [rows_of(e, later_chunk, later) for e in ahead],
            out_specs=[units(heads)] + [units(sent)] * (n - 1),
        ),
        out_shape=[out(heads)] + [out(sent)] * (n - 1),
        compiler_params=params(),
        cost_estimate=pl.CostEstimate(
            flops=4 * clips * groups * (slots * GROUP) ** 2 * heads * E,
            bytes_accessed=16 * clips * slots * rows * heads * E,
            transcendentals=clips * groups * (slots * GROUP) ** 2 * heads,
        ),
        name="temporal",
    )(me, bias, action, projected, *arrived, *([projected] * len(ahead)))


def combine_kernel(n, me_ref, spatial_ref, *refs):
    parts, out_ref = refs[:n], refs[-1]
    heads, _, _, rows, _ = parts[0].shape
    for e in range(n):
        at = pl.ds(pl.multiple_of(lax.rem(me_ref[0] + n - e, n) * rows, rows), rows)
        for h in range(heads):
            cut = slice(h * E, (h + 1) * E)
            one, other = spatial_ref[0, :, at, cut], parts[e][h, 0]
            total = one.astype(jnp.float32) + other.astype(jnp.float32)
            out_ref[0, :, at, cut] = total.astype(jnp.bfloat16)


def combine(mixed, spatial, parts, me, n, chunk, width):
    clips, frames, patches, cols = spatial.shape
    rows = patches // n
    heads = cols // E
    part = pl.BlockSpec((heads, 1, frames, rows, E), lambda c, me_ref: (0, c, 0, 0, 0))
    before = [] if mixed is None else [mixed]
    return pl.pallas_call(
        functools.partial(combine_kernel, n),
        grid_spec=pltpu.PrefetchScalarGridSpec(
            num_scalar_prefetch=1,
            grid=(clips,),
            in_specs=[pl.BlockSpec((1, frames, patches, cols), lambda c, me_ref: (c, 0, 0, 0))]
            + [part] * n
            + [pl.BlockSpec(memory_space=pl.ANY)] * len(before),
            out_specs=pl.BlockSpec((1, frames, patches, cols), lambda c, me_ref: (c, 0, 0, chunk)),
        ),
        out_shape=jax.ShapeDtypeStruct((clips, frames, patches, width), jnp.bfloat16),
        input_output_aliases={n + 2: 0} if before else {},
        compiler_params=params(),
        cost_estimate=pl.CostEstimate(
            flops=clips * frames * patches * cols,
            bytes_accessed=6 * clips * frames * patches * cols,
            transcendentals=0,
        ),
        name="combine",
    )(me, spatial, *parts, *before)


def after(x, *others):
    return lax.optimization_barrier((x, *others))[0]


def chunk_sizes(heads):
    size = max(c for c in range(1, max(1, heads // CHUNKS) + 1) if heads % c == 0)
    return [size] * (heads // size)


def local(n, projected, codes, action_weight, clip_ids, frame_map, segments):
    _, clips, frames, patches, width = projected.shape
    slots = frame_map.shape[0]
    heads = width // E
    sizes = chunk_sizes(heads)
    chunks = len(sizes)
    starts = [sum(sizes[:j]) for j in range(chunks)]
    me_scalar = lax.axis_index("frame")
    me = me_scalar.astype(jnp.int32)[None]
    far_first = sorted(range(1, n), key=lambda d: abs(d - n // 2))

    def send(x, d):
        return lax.ppermute(x, "frame", [(i, (i + d) % n) for i in range(n)])

    def exchange(outgoing):
        got = {e: send(outgoing[e - 1], e) for e in far_first}
        return [got[e] for e in range(1, n)]

    first = {e: pack(projected, me, n, [e], 0, sizes[0])[0] for e in far_first}
    arrived = [exchange([first[e] for e in range(1, n)])]
    if chunks > 1:
        at = starts[1] // sizes[1]
        arrived.append(exchange(pack(projected, me, n, range(1, n), at, sizes[1])))
    else:
        arrived.append(None)

    source = lax.rem(me_scalar - jnp.arange(n) + n, n)
    order = (source[:, None] * frames + jnp.arange(frames)[None, :]).reshape(-1)
    time_of = jnp.sum(
        jnp.where(order[:, None] == jnp.arange(slots)[None, :], frame_map[None, :], 0), axis=-1
    )
    at_time = time_of[:, None] == jnp.arange(slots, dtype=jnp.int32)[None, :]
    seg_slot = jnp.sum(jnp.where(at_time[None], segments[:, None, :], 0), axis=-1)
    allowed = (time_of[None, :] <= time_of[:, None])[None] & (
        seg_slot[:, None, :] == seg_slot[:, :, None]
    )
    row = jnp.arange(slots * GROUP)
    same_patch = (row[:, None] % GROUP) == (row[None, :] % GROUP)
    wide = jnp.repeat(jnp.repeat(allowed, GROUP, axis=1), GROUP, axis=2)
    bias = jnp.where(wide & same_patch[None], 0.0, -1e30).astype(jnp.float32)

    all_codes = lax.all_gather(codes, "dp", axis=0, tiled=True)
    owned = lax.axis_index("dp") * clips + jnp.arange(clips, dtype=jnp.int32)
    select = (clip_ids[:, None] == owned[None, :]).astype(jnp.float32)
    by_clip = jnp.einsum("ic,ifa->cfa", select, all_codes, precision=HIGHEST)
    codes_slot = jnp.einsum(
        "st,cta->csa", at_time.astype(jnp.float32), by_clip, precision=HIGHEST
    )
    action = jnp.einsum("csa,ad->csd", codes_slot, action_weight, precision=HIGHEST)

    places = [start // size for start, size in zip(starts, sizes)] + [0] * AHEAD
    sizes = sizes + [0] * AHEAD
    spatial, own = [], []
    for j in range(chunks):
        while len(spatial) < min(j + 2, chunks):
            i = len(spatial)
            spatial.append(spatial_attention(projected, places[i], sizes[i] * E))
        ahead = j + AHEAD
        done = temporal_attention(
            projected,
            arrived[j],
            sizes[j - AHEAD] if j >= AHEAD else 0,
            bias,
            action,
            after(me, *spatial),
            n,
            places[j],
            sizes[j],
            places[ahead],
            sizes[ahead],
        )
        own.append(done[0])
        arrived.append(exchange(done[1:]))
    mixed = None
    for j in range(chunks):
        parts = [own[j]] + arrived[j + AHEAD]
        mixed = combine(mixed, spatial[j], parts, me, n, places[j], width)
    return mixed


def solution(mesh):
    return jax.shard_map(
        functools.partial(local, mesh.shape["frame"]),
        mesh=mesh,
        in_specs=(
            P(None, "dp", "frame", None, "mp"),
            P("dp", None, None),
            P(None, "mp"),
            P(),
            P(),
            P("dp", None),
        ),
        out_specs=P("dp", "frame", None, "mp"),
        check_vma=False,
    )
```

```python
import functools
import math

import jax
import jax.numpy as jnp
from jax import lax
from jax.experimental import pallas as pl
from jax.experimental.pallas import tpu as pltpu
from jax.sharding import PartitionSpec as P

E = 128
GROUP = 16
SHARES = (4, 4, 4, 4, 4)
AHEAD = 2
EPISODES = 3
HIGHEST = lax.Precision.HIGHEST
VMEM = 48 * 1024 * 1024


def params():
    return pltpu.CompilerParams(vmem_limit_bytes=VMEM)


def pieces(start, heads):
    size = math.gcd(start, heads)
    return heads // size, size, start // size


def spatial_kernel(q_ref, k_ref, v_ref, o_ref):
    heads = q_ref.shape[-1] // E
    for h in range(heads):
        cols = slice(h * E, (h + 1) * E)
        q, k, v = q_ref[0, 0, 0, :, cols], k_ref[0, 0, 0, :, cols], v_ref[0, 0, 0, :, cols]
        s = lax.dot_general(q, k, (((1,), (1,)), ((), ())), preferred_element_type=jnp.float32)
        s = s * (1.0 / E**0.5)
        w = jnp.exp(s - jnp.max(s, axis=-1, keepdims=True))
        p = (w * (1.0 / jnp.sum(w, axis=-1, keepdims=True))).astype(jnp.bfloat16)
        o = jnp.dot(p, v, preferred_element_type=jnp.float32)
        o_ref[0, 0, :, cols] = o.astype(jnp.bfloat16)


def spatial_attention(projected, start, heads):
    _, clips, frames, patches, _ = projected.shape
    count, size, first = pieces(start, heads)
    cols = heads * E
    spec = lambda which: pl.BlockSpec(
        (1, 1, 1, patches, size * E), lambda c, f, i: (which, c, f, 0, first + i)
    )
    return pl.pallas_call(
        spatial_kernel,
        grid=(clips, frames, count),
        in_specs=[spec(0), spec(1), spec(2)],
        out_specs=pl.BlockSpec((1, 1, patches, size * E), lambda c, f, i: (c, f, 0, i)),
        out_shape=jax.ShapeDtypeStruct((clips, frames, patches, cols), jnp.bfloat16),
        compiler_params=params(),
        cost_estimate=pl.CostEstimate(
            flops=4 * clips * frames * patches * patches * cols,
            bytes_accessed=8 * clips * frames * patches * cols,
            transcendentals=clips * frames * patches * patches * (cols // E),
        ),
        name="spatial",
    )(projected, projected, projected)


class Plan:
    def __init__(self, n, frames, patches, heads):
        ends = [round(sum(SHARES[: j + 1]) * heads / sum(SHARES)) for j in range(len(SHARES))]
        self.chunks = [(a, b - a) for a, b in zip([0] + ends, ends) if b > a]
        self.n, self.frames = n, frames
        self.groups = patches // n // GROUP
        self.halved = n == 4 and self.groups == 2 and len({c[1] for c in self.chunks}) == 1
        self.slots = n * frames - EPISODES

    def heads(self, j):
        return self.chunks[j][1] if 0 <= j < len(self.chunks) else 0

    def slotted(self, k):
        return self.halved and self.heads(k) > 0 and self.heads(k - AHEAD) > 0

    def parts(self, k, m):
        full = self.groups * self.frames
        sizes = {}
        if self.slotted(k) and m > 1:
            sizes["kv"] = 2 * self.heads(k) * full
            sizes["slots"] = self.heads(k) * self.slots
        else:
            if self.heads(k):
                sizes["qkv"] = 3 * self.heads(k) * full
            if self.heads(k - AHEAD):
                sizes["o"] = self.heads(k - AHEAD) * full
            if m == 1 and self.slotted(k + AHEAD):
                sizes["ql"] = 2 * self.heads(k + AHEAD) * self.frames
            if m == 1 and self.slotted(k - AHEAD):
                sizes["ol"] = 2 * self.heads(k - AHEAD) * self.frames
        at, total = {}, 0
        for name, size in sizes.items():
            at[name] = total
            total += size
        return at, total

    def tile(self, i, g):
        return (i * self.groups + g) * self.frames


def rows_of(g):
    return pl.ds(pl.multiple_of(g * GROUP, GROUP), GROUP)


def head_cols(refs, h):
    size = refs[0].shape[-1] // E
    return refs[h // size], slice(h % size * E, (h % size + 1) * E)


def write_qkv(plan, heads, which, source, out, at):
    for i, a in enumerate(which):
        for h in range(heads):
            x, cut = head_cols(source, h)
            for g in range(plan.groups):
                to = at + plan.tile(i * heads + h, g)
                rows = slice(g * GROUP, (g + 1) * GROUP)
                out[to : to + plan.frames, 0] = x[a, 0, :, rows, cut]


def write_local_queries(plan, heads, parity, sources, out, at):
    for c, source in enumerate(sources):
        for h in range(heads):
            x, cut = head_cols(source, h)
            to = at + (c * heads + h) * plan.frames
            out[to : to + plan.frames, 0] = x[0, 0, :, rows_of(1 - parity), cut]


def pack_kernel(plan, k, m, me_ref, *refs):
    at, _ = plan.parts(k, m)
    count = len(refs) - 1
    blocks = pieces(*plan.chunks[k])[0]
    write_qkv(plan, plan.heads(k), range(3), refs[:blocks], refs[-1], at["qkv"])
    if "ql" in at:
        later = refs[blocks:count]
        half = len(later) // 2
        sources = [later[:half], later[half:]]
        parity = lax.rem(me_ref[0], 2)
        write_local_queries(plan, plan.heads(k + AHEAD), parity, sources, refs[-1], at["ql"])


def peer_rows(plan, chunk, m, arrays, first_array, patches):
    count, size, first = pieces(*chunk)
    return [
        pl.BlockSpec(
            (arrays, 1, plan.frames, patches // plan.n, size * E),
            lambda c, me_ref, *_, i=i: (first_array, c, 0, me_ref[0] ^ m, first + i),
        )
        for i in range(count)
    ]


def tiles(total):
    return pl.BlockSpec((total, 1, GROUP, E), lambda c, *_: (0, c, 0, 0))


def pack(plan, projected, me, k, m):
    _, clips, _, patches, _ = projected.shape
    at, total = plan.parts(k, m)
    specs = peer_rows(plan, plan.chunks[k], m, 3, 1, patches)
    if "ql" in at:
        for peer in (2, 3):
            specs += peer_rows(plan, plan.chunks[k + AHEAD], peer, 1, 3, patches)
    return pl.pallas_call(
        functools.partial(pack_kernel, plan, k, m),
        grid_spec=pltpu.PrefetchScalarGridSpec(
            num_scalar_prefetch=1, grid=(clips,), in_specs=specs, out_specs=tiles(total)
        ),
        out_shape=jax.ShapeDtypeStruct((total, clips, GROUP, E), jnp.bfloat16),
        compiler_params=params(),
        cost_estimate=pl.CostEstimate(
            flops=0, bytes_accessed=4 * total * clips * GROUP * E, transcendentals=0
        ),
        name="pack",
    )(me, *([projected] * len(specs)))


def slot(plan, base, h, i):
    return base + h * plan.slots + jnp.minimum(i, plan.slots - 1)


def temporal_kernel(plan, j, me_ref, rank_ref, alone_ref, kept_ref, *refs):
    n, frames, groups = plan.n, plan.frames, plan.groups
    slots, heads = n * frames, plan.heads(j)
    half = 2 * frames
    c = pl.program_id(0)
    parity = lax.rem(me_ref[0], 2)
    rank = lambda x: rank_ref[c * slots + x]
    alone = lambda x: alone_ref[c * slots + x]
    kept_here, kept_there = kept_ref[c * 2], kept_ref[c * 2 + 1]
    bias_ref, action_ref, refs = refs[0], refs[1], refs[2:]
    bias = bias_ref[0]
    start = plan.chunks[j][0]
    own, refs = refs[: pieces(*plan.chunks[j])[0]], refs[pieces(*plan.chunks[j])[0] :]
    arrived, refs = refs[: n - 1], refs[n - 1 :]
    k = j + AHEAD
    ahead = []
    if plan.heads(k):
        blocks = pieces(*plan.chunks[k])[0]
        for _ in range(1, n):
            ahead.append(refs[:blocks])
            refs = refs[blocks:]
    beyond = []
    if "ql" in plan.parts(k, 1)[0]:
        blocks = pieces(*plan.chunks[k + AHEAD])[0]
        for _ in range(2):
            beyond.append(refs[:blocks])
            refs = refs[blocks:]
    own_out, outs = refs[0], refs[1:]
    came = [plan.parts(j, m)[0] for m in range(1, n)]
    goes = [plan.parts(k, m)[0] for m in range(1, n)]
    slots_in, slots_out = plan.slotted(j), plan.slotted(k)

    for h in range(heads):
        x, cut = head_cols(own, h)
        for r in range(groups):
            g = lax.rem(parity + r, 2) if plan.halved else r
            rows = rows_of(g) if plan.halved else slice(g * GROUP, (g + 1) * GROUP)

            def array(a):
                parts = [x[a, 0, :, rows, cut]]
                for m in range(1, n):
                    at = came[m - 1]
                    if slots_in and m > 1 and a == 0:
                        if m == 2:
                            for y in range(half, slots):
                                to = slot(plan, at["slots"], h, rank(y))
                                parts.append(arrived[1 + r][pl.ds(to, 1), 0])
                        continue
                    i = (a * heads + h) if "qkv" in at else ((a - 1) * heads + h)
                    to = at["qkv" if "qkv" in at else "kv"] + plan.tile(i, g)
                    parts.append(arrived[m - 1][pl.ds(to, frames), 0])
                return jnp.concatenate(parts, axis=0)

            q = array(0).reshape(slots * GROUP, E)
            key = array(1).reshape(slots * GROUP, E)
            action = action_ref[0, :, (start + h) * E : (start + h + 1) * E].reshape(slots, 1, E)
            v = (array(2).astype(jnp.float32) + action).astype(jnp.bfloat16)
            v = v.reshape(slots * GROUP, E)
            s = lax.dot_general(
                q, key, (((1,), (1,)), ((), ())), preferred_element_type=jnp.float32
            )
            s = s * (1.0 / E**0.5) + bias
            w = jnp.exp(s - jnp.max(s, axis=-1, keepdims=True))
            p = (w * (1.0 / jnp.sum(w, axis=-1, keepdims=True))).astype(jnp.bfloat16)
            o = jnp.dot(p, v, preferred_element_type=jnp.float32).astype(jnp.bfloat16)
            o = o.reshape(slots, GROUP, E)
            own_out[pl.ds(plan.tile(h, g), frames), 0] = o[:frames]
            for m in range(1, n):
                if slots_out and m > 1:
                    continue
                to = goes[m - 1]["o"] + plan.tile(h, g)
                outs[m - 1][pl.ds(to, frames), 0] = o[m * frames : (m + 1) * frames]
            if slots_out:
                for y in range(half, slots):

                    @pl.when(alone(y) == 0)
                    def _():
                        to = slot(plan, goes[1]["slots"], h, kept_here + rank(y))
                        outs[1 + r][pl.ds(to, 1), 0] = o[y : y + 1]

    if ahead:
        later = plan.heads(k)
        for m in range(1, n):
            at = goes[m - 1]
            if "qkv" in at:
                write_qkv(plan, later, range(3), ahead[m - 1], outs[m - 1], at["qkv"])
                continue
            write_qkv(plan, later, (1, 2), ahead[m - 1], outs[m - 1], at["kv"])
            for h in range(later):
                x, cut = head_cols(ahead[m - 1], h)
                for y in range(half):
                    local = came[0]["ql"] + ((m ^ 1) - 2) * later * frames + h * frames + y - frames

                    @pl.when(alone(y) == 0)
                    def _():
                        to = slot(plan, at["slots"], h, rank(y))
                        if y < frames:
                            outs[m - 1][pl.ds(to, 1), 0] = x[0, 0, y : y + 1, rows_of(parity), cut]
                        else:
                            outs[m - 1][pl.ds(to, 1), 0] = arrived[0][local : local + 1, 0]

    if beyond:
        write_local_queries(plan, plan.heads(k + AHEAD), parity, beyond, outs[0], goes[0]["ql"])
    if "ol" in goes[0]:
        for i in range(2):
            for h in range(plan.heads(j - AHEAD)):
                for y in range(frames):
                    at = slot(plan, came[1 + i]["slots"], h, kept_there + rank(frames + y))
                    to = goes[0]["ol"] + (i * plan.heads(j - AHEAD) + h) * frames + y
                    outs[0][to : to + 1, 0] = arrived[1 + i][pl.ds(at, 1), 0]


def temporal_attention(plan, projected, arrived, bias, action, me, tables, j):
    _, clips, frames, patches, _ = projected.shape
    n, k, heads = plan.n, j + AHEAD, plan.heads(j)
    slots = n * frames
    own = peer_rows(plan, plan.chunks[j], 0, 3, 1, patches)
    ahead = []
    if plan.heads(k):
        for m in range(1, n):
            ahead += peer_rows(plan, plan.chunks[k], m, 3, 1, patches)
    if "ql" in plan.parts(k, 1)[0]:
        for peer in (2, 3):
            ahead += peer_rows(plan, plan.chunks[k + AHEAD], peer, 1, 3, patches)
    totals = [heads * plan.groups * frames] + [plan.parts(k, m)[1] for m in range(1, n)]
    return pl.pallas_call(
        functools.partial(temporal_kernel, plan, j),
        grid_spec=pltpu.PrefetchScalarGridSpec(
            num_scalar_prefetch=4,
            grid=(clips,),
            in_specs=[
                pl.BlockSpec((1, slots * GROUP, slots * GROUP), lambda c, *_: (c, 0, 0)),
                pl.BlockSpec((1, slots, action.shape[2]), lambda c, *_: (c, 0, 0)),
            ]
            + own
            + [tiles(x.shape[0]) for x in arrived]
            + ahead,
            out_specs=[tiles(total) for total in totals],
        ),
        out_shape=[
            jax.ShapeDtypeStruct((total, clips, GROUP, E), jnp.bfloat16) for total in totals
        ],
        compiler_params=params(),
        cost_estimate=pl.CostEstimate(
            flops=4 * clips * plan.groups * (slots * GROUP) ** 2 * heads * E,
            bytes_accessed=4 * clips * sum(totals) * GROUP * E,
            transcendentals=clips * plan.groups * (slots * GROUP) ** 2 * heads,
        ),
        name="temporal",
    )(
        me,
        *tables,
        bias,
        action,
        *([projected] * len(own)),
        *arrived,
        *([projected] * len(ahead)),
    )


def combine_kernel(plan, j, me_ref, rank_ref, alone_ref, kept_ref, spatial_ref, *refs):
    n, frames, heads = plan.n, plan.frames, plan.heads(j)
    own, back, refs = refs[0], refs[1:n], refs[n:]
    out_ref = refs[-1]
    c = pl.program_id(0)
    me = me_ref[0]
    parity = lax.rem(me, 2)
    slotted = plan.slotted(j + AHEAD)
    came = [plan.parts(j + AHEAD, m)[0] for m in range(1, n)]
    share = plan.groups * GROUP
    kept_there = kept_ref[c * 2 + 1]

    def put(f, h, at, temporal):
        rows = pl.ds(pl.multiple_of(at, GROUP), temporal.shape[0])
        cut = slice(h * E, (h + 1) * E)
        total = spatial_ref[0, f, rows, cut].astype(jnp.float32) + temporal.astype(jnp.float32)
        out_ref[0, f, rows, cut] = total.astype(jnp.bfloat16)

    for h in range(heads):
        for f in range(frames):
            for m in range(n):
                row = (me ^ m) * share
                if slotted and m > 1:
                    to = slot(
                        plan,
                        came[m - 1]["slots"],
                        h,
                        kept_there + rank_ref[c * n * frames + f],
                    )
                    put(f, h, row + parity * GROUP, back[m - 1][pl.ds(to, 1), 0][0])
                    local = plan.parts(j + 2 * AHEAD, 1)[0]["ol"]
                    local += (((m ^ 1) - 2) * heads + h) * frames + f
                    put(f, h, row + (1 - parity) * GROUP, refs[0][local, 0])
                    continue
                x = own if m == 0 else back[m - 1]
                base = 0 if m == 0 else came[m - 1]["o"]
                for g in range(plan.groups):
                    put(f, h, row + g * GROUP, x[base + plan.tile(h, g) + f, 0])
    if slotted:
        blocks = pieces(*plan.chunks[j])[0]
        values, action_ref = refs[1 : 1 + blocks], refs[1 + blocks]
        start = plan.chunks[j][0]
        for f in range(frames):

            @pl.when(alone_ref[c * n * frames + f] == 1)
            def _():
                for h in range(heads):
                    x, cut = head_cols(values, h)
                    action = action_ref[0, f : f + 1, (start + h) * E : (start + h + 1) * E]
                    v = x[0, 0, f, :, cut].astype(jnp.float32) + action
                    put(f, h, 0, v.astype(jnp.bfloat16))


def combine(plan, mixed, spatial, own, back, handed, projected, action, me, tables, j, width):
    clips, frames, patches, cols = spatial.shape
    n = plan.n
    start, heads = plan.chunks[j]
    count, size, first = pieces(start, heads)
    whole = pl.BlockSpec((1, frames, patches, cols), lambda c, *_: (c, 0, 0, 0))
    arrays, specs = [spatial, own, *back], [whole] + [tiles(x.shape[0]) for x in (own, *back)]
    if plan.slotted(j + AHEAD):
        arrays += [handed] + [projected] * count + [action]
        specs += [tiles(handed.shape[0])]
        specs += [
            pl.BlockSpec(
                (1, 1, frames, patches, size * E), lambda c, *_, i=i: (5, c, 0, 0, first + i)
            )
            for i in range(count)
        ]
        specs += [pl.BlockSpec((1, action.shape[1], action.shape[2]), lambda c, *_: (c, 0, 0))]
    if mixed is not None:
        arrays += [mixed]
        specs += [pl.BlockSpec(memory_space=pl.ANY)]
    assert start % heads == 0
    return pl.pallas_call(
        functools.partial(combine_kernel, plan, j),
        grid_spec=pltpu.PrefetchScalarGridSpec(
            num_scalar_prefetch=4,
            grid=(clips,),
            in_specs=specs,
            out_specs=pl.BlockSpec(
                (1, frames, patches, cols), lambda c, *_: (c, 0, 0, start // heads)
            ),
        ),
        out_shape=jax.ShapeDtypeStruct((clips, frames, patches, width), jnp.bfloat16),
        input_output_aliases={} if mixed is None else {3 + len(arrays): 0},
        compiler_params=params(),
        cost_estimate=pl.CostEstimate(
            flops=clips * frames * patches * cols,
            bytes_accessed=6 * clips * frames * patches * cols,
            transcendentals=0,
        ),
        name="combine",
    )(me, *tables, *arrays)


def after(x, *others):
    return lax.optimization_barrier((x, *others))[0]


def local(n, projected, codes, action_weight, clip_ids, frame_map, segments):
    _, clips, frames, patches, width = projected.shape
    slots = frame_map.shape[0]
    plan = Plan(n, frames, patches, width // E)
    count = len(plan.chunks)
    me_scalar = lax.axis_index("frame").astype(jnp.int32)
    me = me_scalar[None]
    order_of_peers = [*range(2, n), 1]

    def send(x, m):
        return lax.ppermute(x, "frame", [(i, i ^ m) for i in range(n)])

    def exchange(outgoing):
        got = {m: send(outgoing[m - 1], m) for m in order_of_peers}
        return [got[m] for m in range(1, n)]

    arrived = []
    for k in range(min(AHEAD, count)):
        packed = {m: pack(plan, projected, me, k, m) for m in order_of_peers}
        arrived.append(exchange([packed[m] for m in range(1, n)]))

    source = me_scalar ^ jnp.arange(n, dtype=jnp.int32)
    order = (source[:, None] * frames + jnp.arange(frames, dtype=jnp.int32)[None, :]).reshape(-1)
    time_of = jnp.sum(
        jnp.where(order[:, None] == jnp.arange(slots)[None, :], frame_map[None, :], 0), axis=-1
    )
    at_time = time_of[:, None] == jnp.arange(slots, dtype=jnp.int32)[None, :]
    seg_slot = jnp.sum(jnp.where(at_time[None], segments[:, None, :], 0), axis=-1)
    allowed = (time_of[None, :] <= time_of[:, None])[None] & (
        seg_slot[:, None, :] == seg_slot[:, :, None]
    )
    row = jnp.arange(slots * GROUP)
    same_patch = (row[:, None] % GROUP) == (row[None, :] % GROUP)
    wide = jnp.repeat(jnp.repeat(allowed, GROUP, axis=1), GROUP, axis=2)
    bias = jnp.where(wide & same_patch[None], 0.0, -1e30).astype(jnp.float32)

    alone = jnp.sum(allowed.astype(jnp.int32), axis=-1) == 1
    half_of = order // (slots // 2)
    before = (half_of[:, None] == half_of[None, :]) & (order[None, :] < order[:, None])
    rank = jnp.sum((before[None] & ~alone[:, None, :]).astype(jnp.int32), axis=-1)
    here = (half_of == half_of[0])[None]
    kept = jnp.stack(
        [jnp.sum((~alone & here).astype(jnp.int32), -1), jnp.sum((~alone & ~here).astype(jnp.int32), -1)],
        axis=-1,
    )
    tables = [rank.reshape(-1), alone.astype(jnp.int32).reshape(-1), kept.reshape(-1)]

    all_codes = lax.all_gather(codes, "dp", axis=0, tiled=True)
    owned = lax.axis_index("dp") * clips + jnp.arange(clips, dtype=jnp.int32)
    select = (clip_ids[:, None] == owned[None, :]).astype(jnp.float32)
    by_clip = jnp.einsum("ic,ifa->cfa", select, all_codes, precision=HIGHEST)
    codes_slot = jnp.einsum(
        "st,cta->csa", at_time.astype(jnp.float32), by_clip, precision=HIGHEST
    )
    action = jnp.einsum("csa,ad->csd", codes_slot, action_weight, precision=HIGHEST)

    spatial, own = [], []
    for j in range(count):
        for early in plan.chunks[len(spatial) : j + 2]:
            spatial.append(spatial_attention(projected, *early))
        done = temporal_attention(
            plan, projected, arrived[j], bias, action, after(me, *spatial), tables, j
        )
        own.append(done[0])
        arrived.append(exchange(done[1:]))
    mixed = None
    for j in range(count):
        handed = arrived[j + 2 * AHEAD][0] if plan.slotted(j + AHEAD) else None
        mixed = combine(
            plan, mixed, spatial[j], own[j], arrived[j + AHEAD], handed, projected, action, me, tables,
            j, width,
        )
    return mixed


def solution(mesh):
    return jax.shard_map(
        functools.partial(local, mesh.shape["frame"]),
        mesh=mesh,
        in_specs=(
            P(None, "dp", "frame", None, "mp"),
            P("dp", None, None),
            P(None, "mp"),
            P(),
            P(),
            P("dp", None),
        ),
        out_specs=P("dp", "frame", None, "mp"),
        check_vma=False,
    )
```

```python
import functools
import math

import jax
import jax.numpy as jnp
from jax import lax
from jax.experimental import pallas as pl
from jax.experimental.pallas import tpu as pltpu
from jax.sharding import PartitionSpec as P

E = 128
GROUP = 16
SHARES = (4, 4, 4, 4, 4)
AHEAD = 2
EPISODES = 3
HIGHEST = lax.Precision.HIGHEST
VMEM = 48 * 1024 * 1024


def params():
    return pltpu.CompilerParams(vmem_limit_bytes=VMEM)


def pieces(start, heads):
    size = math.gcd(start, heads)
    return heads // size, size, start // size


def spatial_kernel(q_ref, k_ref, v_ref, o_ref):
    heads = q_ref.shape[-1] // E
    for h in range(heads):
        cols = slice(h * E, (h + 1) * E)
        q, k, v = q_ref[0, 0, 0, :, cols], k_ref[0, 0, 0, :, cols], v_ref[0, 0, 0, :, cols]
        s = lax.dot_general(q, k, (((1,), (1,)), ((), ())), preferred_element_type=jnp.float32)
        s = s * (1.0 / E**0.5)
        w = jnp.exp(s - jnp.max(s, axis=-1, keepdims=True))
        p = (w * (1.0 / jnp.sum(w, axis=-1, keepdims=True))).astype(jnp.bfloat16)
        o = jnp.dot(p, v, preferred_element_type=jnp.float32)
        o_ref[0, 0, :, cols] = o.astype(jnp.bfloat16)


def spatial_attention(projected, start, heads):
    _, clips, frames, patches, _ = projected.shape
    count, size, first = pieces(start, heads)
    cols = heads * E
    spec = lambda which: pl.BlockSpec(
        (1, 1, 1, patches, size * E), lambda c, f, i: (which, c, f, 0, first + i)
    )
    return pl.pallas_call(
        spatial_kernel,
        grid=(clips, frames, count),
        in_specs=[spec(0), spec(1), spec(2)],
        out_specs=pl.BlockSpec((1, 1, patches, size * E), lambda c, f, i: (c, f, 0, i)),
        out_shape=jax.ShapeDtypeStruct((clips, frames, patches, cols), jnp.bfloat16),
        compiler_params=params(),
        cost_estimate=pl.CostEstimate(
            flops=4 * clips * frames * patches * patches * cols,
            bytes_accessed=8 * clips * frames * patches * cols,
            transcendentals=clips * frames * patches * patches * (cols // E),
        ),
        name="spatial",
    )(projected, projected, projected)


class Plan:
    def __init__(self, n, frames, patches, heads):
        ends = [round(sum(SHARES[: j + 1]) * heads / sum(SHARES)) for j in range(len(SHARES))]
        self.chunks = [(a, b - a) for a, b in zip([0] + ends, ends) if b > a]
        self.n, self.frames = n, frames
        self.groups = patches // n // GROUP
        self.halved = n == 4 and self.groups == 2 and len({c[1] for c in self.chunks}) == 1
        self.slots = n * frames - EPISODES

    def heads(self, j):
        return self.chunks[j][1] if 0 <= j < len(self.chunks) else 0

    def slotted(self, k):
        return self.halved and self.heads(k) > 0 and self.heads(k - AHEAD) > 0

    def parts(self, k, m):
        full = self.groups * self.frames
        sizes = {}
        if self.slotted(k) and m > 1:
            sizes["kv"] = 2 * self.heads(k) * full
            sizes["slots"] = self.heads(k) * self.slots
        else:
            if self.heads(k):
                sizes["qkv"] = 3 * self.heads(k) * full
            if self.heads(k - AHEAD):
                sizes["o"] = self.heads(k - AHEAD) * full
            if m == 1 and self.slotted(k + AHEAD):
                sizes["ql"] = 2 * self.heads(k + AHEAD) * self.frames
            if m == 1 and self.slotted(k - AHEAD):
                sizes["ol"] = 2 * self.heads(k - AHEAD) * self.frames
        at, total = {}, 0
        for name, size in sizes.items():
            at[name] = total
            total += size
        return at, total

    def tile(self, i, g):
        return (i * self.groups + g) * self.frames


def rows_of(g):
    return pl.ds(pl.multiple_of(g * GROUP, GROUP), GROUP)


def head_cols(refs, h):
    size = refs[0].shape[-1] // E
    return refs[h // size], slice(h % size * E, (h % size + 1) * E)


def write_qkv(plan, heads, which, source, out, at):
    for i, a in enumerate(which):
        for h in range(heads):
            x, cut = head_cols(source, h)
            for g in range(plan.groups):
                to = at + plan.tile(i * heads + h, g)
                rows = slice(g * GROUP, (g + 1) * GROUP)
                out[to : to + plan.frames, 0] = x[a, 0, :, rows, cut]


def write_local_queries(plan, heads, parity, sources, out, at):
    for c, source in enumerate(sources):
        for h in range(heads):
            x, cut = head_cols(source, h)
            to = at + (c * heads + h) * plan.frames
            out[to : to + plan.frames, 0] = x[0, 0, :, rows_of(1 - parity), cut]


def pack_kernel(plan, k, m, me_ref, *refs):
    at, _ = plan.parts(k, m)
    count = len(refs) - 1
    blocks = pieces(*plan.chunks[k])[0]
    write_qkv(plan, plan.heads(k), range(3), refs[:blocks], refs[-1], at["qkv"])
    if "ql" in at:
        later = refs[blocks:count]
        half = len(later) // 2
        sources = [later[:half], later[half:]]
        parity = lax.rem(me_ref[0], 2)
        write_local_queries(plan, plan.heads(k + AHEAD), parity, sources, refs[-1], at["ql"])


def peer_rows(plan, chunk, m, arrays, first_array, patches):
    count, size, first = pieces(*chunk)
    return [
        pl.BlockSpec(
            (arrays, 1, plan.frames, patches // plan.n, size * E),
            lambda c, me_ref, *_, i=i: (first_array, c, 0, me_ref[0] ^ m, first + i),
        )
        for i in range(count)
    ]


def tiles(total):
    return pl.BlockSpec((total, 1, GROUP, E), lambda c, *_: (0, c, 0, 0))


def pack(plan, projected, me, k, m):
    _, clips, _, patches, _ = projected.shape
    at, total = plan.parts(k, m)
    specs = peer_rows(plan, plan.chunks[k], m, 3, 1, patches)
    if "ql" in at:
        for peer in (2, 3):
            specs += peer_rows(plan, plan.chunks[k + AHEAD], peer, 1, 3, patches)
    return pl.pallas_call(
        functools.partial(pack_kernel, plan, k, m),
        grid_spec=pltpu.PrefetchScalarGridSpec(
            num_scalar_prefetch=1, grid=(clips,), in_specs=specs, out_specs=tiles(total)
        ),
        out_shape=jax.ShapeDtypeStruct((total, clips, GROUP, E), jnp.bfloat16),
        compiler_params=params(),
        cost_estimate=pl.CostEstimate(
            flops=0, bytes_accessed=4 * total * clips * GROUP * E, transcendentals=0
        ),
        name="pack",
    )(me, *([projected] * len(specs)))


def slot(plan, base, h, i):
    return base + h * plan.slots + jnp.minimum(i, plan.slots - 1)


def temporal_kernel(plan, j, me_ref, rank_ref, alone_ref, kept_ref, *refs):
    n, frames, groups = plan.n, plan.frames, plan.groups
    slots, heads = n * frames, plan.heads(j)
    half = 2 * frames
    c = pl.program_id(0)
    parity = lax.rem(me_ref[0], 2)
    rank = lambda x: rank_ref[c * slots + x]
    alone = lambda x: alone_ref[c * slots + x]
    kept_here, kept_there = kept_ref[c * 2], kept_ref[c * 2 + 1]
    bias_ref, action_ref, refs = refs[0], refs[1], refs[2:]
    bias = bias_ref[0]
    start = plan.chunks[j][0]
    own, refs = refs[: pieces(*plan.chunks[j])[0]], refs[pieces(*plan.chunks[j])[0] :]
    arrived, refs = refs[: n - 1], refs[n - 1 :]
    k = j + AHEAD
    ahead = []
    if plan.heads(k):
        blocks = pieces(*plan.chunks[k])[0]
        for _ in range(1, n):
            ahead.append(refs[:blocks])
            refs = refs[blocks:]
    beyond = []
    if "ql" in plan.parts(k, 1)[0]:
        blocks = pieces(*plan.chunks[k + AHEAD])[0]
        for _ in range(2):
            beyond.append(refs[:blocks])
            refs = refs[blocks:]
    own_out, outs = refs[0], refs[1:]
    came = [plan.parts(j, m)[0] for m in range(1, n)]
    goes = [plan.parts(k, m)[0] for m in range(1, n)]
    slots_in, slots_out = plan.slotted(j), plan.slotted(k)

    for h in range(heads):
        x, cut = head_cols(own, h)
        for r in range(groups):
            g = lax.rem(parity + r, 2) if plan.halved else r
            rows = rows_of(g) if plan.halved else slice(g * GROUP, (g + 1) * GROUP)

            def array(a):
                parts = [x[a, 0, :, rows, cut]]
                for m in range(1, n):
                    at = came[m - 1]
                    if slots_in and m > 1 and a == 0:
                        if m == 2:
                            for y in range(half, slots):
                                to = slot(plan, at["slots"], h, rank(y))
                                parts.append(arrived[1 + r][pl.ds(to, 1), 0])
                        continue
                    i = (a * heads + h) if "qkv" in at else ((a - 1) * heads + h)
                    to = at["qkv" if "qkv" in at else "kv"] + plan.tile(i, g)
                    parts.append(arrived[m - 1][pl.ds(to, frames), 0])
                return jnp.concatenate(parts, axis=0)

            q = array(0).reshape(slots * GROUP, E)
            key = array(1).reshape(slots * GROUP, E)
            action = action_ref[0, :, (start + h) * E : (start + h + 1) * E].reshape(slots, 1, E)
            v = (array(2).astype(jnp.float32) + action).astype(jnp.bfloat16)
            v = v.reshape(slots * GROUP, E)
            s = lax.dot_general(
                q, key, (((1,), (1,)), ((), ())), preferred_element_type=jnp.float32
            )
            s = s * (1.0 / E**0.5) + bias
            w = jnp.exp(s - jnp.max(s, axis=-1, keepdims=True))
            p = (w * (1.0 / jnp.sum(w, axis=-1, keepdims=True))).astype(jnp.bfloat16)
            o = jnp.dot(p, v, preferred_element_type=jnp.float32).astype(jnp.bfloat16)
            o = o.reshape(slots, GROUP, E)
            own_out[pl.ds(plan.tile(h, g), frames), 0] = o[:frames]
            for m in range(1, n):
                if slots_out and m > 1:
                    continue
                to = goes[m - 1]["o"] + plan.tile(h, g)
                outs[m - 1][pl.ds(to, frames), 0] = o[m * frames : (m + 1) * frames]
            if slots_out:
                for y in range(half, slots):

                    @pl.when(alone(y) == 0)
                    def _():
                        to = slot(plan, goes[1]["slots"], h, kept_here + rank(y))
                        outs[1 + r][pl.ds(to, 1), 0] = o[y : y + 1]

    if ahead:
        later = plan.heads(k)
        for m in range(1, n):
            at = goes[m - 1]
            if "qkv" in at:
                write_qkv(plan, later, range(3), ahead[m - 1], outs[m - 1], at["qkv"])
                continue
            write_qkv(plan, later, (1, 2), ahead[m - 1], outs[m - 1], at["kv"])
            for h in range(later):
                x, cut = head_cols(ahead[m - 1], h)
                for y in range(half):
                    local = came[0]["ql"] + ((m ^ 1) - 2) * later * frames + h * frames + y - frames

                    @pl.when(alone(y) == 0)
                    def _():
                        to = slot(plan, at["slots"], h, rank(y))
                        if y < frames:
                            outs[m - 1][pl.ds(to, 1), 0] = x[0, 0, y : y + 1, rows_of(parity), cut]
                        else:
                            outs[m - 1][pl.ds(to, 1), 0] = arrived[0][local : local + 1, 0]

    if beyond:
        write_local_queries(plan, plan.heads(k + AHEAD), parity, beyond, outs[0], goes[0]["ql"])
    if "ol" in goes[0]:
        for i in range(2):
            for h in range(plan.heads(j - AHEAD)):
                for y in range(frames):
                    at = slot(plan, came[1 + i]["slots"], h, kept_there + rank(frames + y))
                    to = goes[0]["ol"] + (i * plan.heads(j - AHEAD) + h) * frames + y
                    outs[0][to : to + 1, 0] = arrived[1 + i][pl.ds(at, 1), 0]


def temporal_attention(plan, projected, arrived, bias, action, me, tables, j):
    _, clips, frames, patches, _ = projected.shape
    n, k, heads = plan.n, j + AHEAD, plan.heads(j)
    slots = n * frames
    own = peer_rows(plan, plan.chunks[j], 0, 3, 1, patches)
    ahead = []
    if plan.heads(k):
        for m in range(1, n):
            ahead += peer_rows(plan, plan.chunks[k], m, 3, 1, patches)
    if "ql" in plan.parts(k, 1)[0]:
        for peer in (2, 3):
            ahead += peer_rows(plan, plan.chunks[k + AHEAD], peer, 1, 3, patches)
    totals = [heads * plan.groups * frames] + [plan.parts(k, m)[1] for m in range(1, n)]
    return pl.pallas_call(
        functools.partial(temporal_kernel, plan, j),
        grid_spec=pltpu.PrefetchScalarGridSpec(
            num_scalar_prefetch=4,
            grid=(clips,),
            in_specs=[
                pl.BlockSpec((1, slots * GROUP, slots * GROUP), lambda c, *_: (c, 0, 0)),
                pl.BlockSpec((1, slots, action.shape[2]), lambda c, *_: (c, 0, 0)),
            ]
            + own
            + [tiles(x.shape[0]) for x in arrived]
            + ahead,
            out_specs=[tiles(total) for total in totals],
        ),
        out_shape=[
            jax.ShapeDtypeStruct((total, clips, GROUP, E), jnp.bfloat16) for total in totals
        ],
        compiler_params=params(),
        cost_estimate=pl.CostEstimate(
            flops=4 * clips * plan.groups * (slots * GROUP) ** 2 * heads * E,
            bytes_accessed=4 * clips * sum(totals) * GROUP * E,
            transcendentals=clips * plan.groups * (slots * GROUP) ** 2 * heads,
        ),
        name="temporal",
    )(
        me,
        *tables,
        bias,
        action,
        *([projected] * len(own)),
        *arrived,
        *([projected] * len(ahead)),
    )


def combine_kernel(plan, j, me_ref, rank_ref, alone_ref, kept_ref, spatial_ref, *refs):
    n, frames, heads = plan.n, plan.frames, plan.heads(j)
    own, back, refs = refs[0], refs[1:n], refs[n:]
    out_ref = refs[-1]
    c = pl.program_id(0)
    me = me_ref[0]
    parity = lax.rem(me, 2)
    slotted = plan.slotted(j + AHEAD)
    came = [plan.parts(j + AHEAD, m)[0] for m in range(1, n)]
    share = plan.groups * GROUP
    kept_there = kept_ref[c * 2 + 1]

    def put(f, h, at, temporal):
        rows = pl.ds(pl.multiple_of(at, GROUP), temporal.shape[0])
        cut = slice(h * E, (h + 1) * E)
        total = spatial_ref[0, f, rows, cut].astype(jnp.float32) + temporal.astype(jnp.float32)
        out_ref[0, f, rows, cut] = total.astype(jnp.bfloat16)

    for h in range(heads):
        for f in range(frames):
            for m in range(n):
                row = (me ^ m) * share
                if slotted and m > 1:
                    to = slot(
                        plan,
                        came[m - 1]["slots"],
                        h,
                        kept_there + rank_ref[c * n * frames + f],
                    )
                    put(f, h, row + parity * GROUP, back[m - 1][pl.ds(to, 1), 0][0])
                    local = plan.parts(j + 2 * AHEAD, 1)[0]["ol"]
                    local += (((m ^ 1) - 2) * heads + h) * frames + f
                    put(f, h, row + (1 - parity) * GROUP, refs[0][local, 0])
                    continue
                x = own if m == 0 else back[m - 1]
                base = 0 if m == 0 else came[m - 1]["o"]
                for g in range(plan.groups):
                    put(f, h, row + g * GROUP, x[base + plan.tile(h, g) + f, 0])
    if slotted:
        blocks = pieces(*plan.chunks[j])[0]
        values, action_ref = refs[1 : 1 + blocks], refs[1 + blocks]
        start = plan.chunks[j][0]
        for f in range(frames):

            @pl.when(alone_ref[c * n * frames + f] == 1)
            def _():
                for h in range(heads):
                    x, cut = head_cols(values, h)
                    action = action_ref[0, f : f + 1, (start + h) * E : (start + h + 1) * E]
                    v = x[0, 0, f, :, cut].astype(jnp.float32) + action
                    put(f, h, 0, v.astype(jnp.bfloat16))


def combine(plan, mixed, spatial, own, back, handed, projected, action, me, tables, j, width):
    clips, frames, patches, cols = spatial.shape
    n = plan.n
    start, heads = plan.chunks[j]
    count, size, first = pieces(start, heads)
    whole = pl.BlockSpec((1, frames, patches, cols), lambda c, *_: (c, 0, 0, 0))
    arrays, specs = [spatial, own, *back], [whole] + [tiles(x.shape[0]) for x in (own, *back)]
    if plan.slotted(j + AHEAD):
        arrays += [handed] + [projected] * count + [action]
        specs += [tiles(handed.shape[0])]
        specs += [
            pl.BlockSpec(
                (1, 1, frames, patches, size * E), lambda c, *_, i=i: (5, c, 0, 0, first + i)
            )
            for i in range(count)
        ]
        specs += [pl.BlockSpec((1, action.shape[1], action.shape[2]), lambda c, *_: (c, 0, 0))]
    if mixed is not None:
        arrays += [mixed]
        specs += [pl.BlockSpec(memory_space=pl.ANY)]
    assert start % heads == 0
    return pl.pallas_call(
        functools.partial(combine_kernel, plan, j),
        grid_spec=pltpu.PrefetchScalarGridSpec(
            num_scalar_prefetch=4,
            grid=(clips,),
            in_specs=specs,
            out_specs=pl.BlockSpec(
                (1, frames, patches, cols), lambda c, *_: (c, 0, 0, start // heads)
            ),
        ),
        out_shape=jax.ShapeDtypeStruct((clips, frames, patches, width), jnp.bfloat16),
        input_output_aliases={} if mixed is None else {3 + len(arrays): 0},
        compiler_params=params(),
        cost_estimate=pl.CostEstimate(
            flops=clips * frames * patches * cols,
            bytes_accessed=6 * clips * frames * patches * cols,
            transcendentals=0,
        ),
        name="combine",
    )(me, *tables, *arrays)


def after(x, *others):
    return lax.optimization_barrier((x, *others))[0]


def local(n, projected, codes, action_weight, clip_ids, frame_map, segments):
    _, clips, frames, patches, width = projected.shape
    slots = frame_map.shape[0]
    plan = Plan(n, frames, patches, width // E)
    count = len(plan.chunks)
    me_scalar = lax.axis_index("frame").astype(jnp.int32)
    me = me_scalar[None]
    order_of_peers = [*range(2, n), 1]

    def send(x, m):
        return lax.ppermute(x, "frame", [(i, i ^ m) for i in range(n)])

    def exchange(outgoing):
        got = {m: send(outgoing[m - 1], m) for m in order_of_peers}
        return [got[m] for m in range(1, n)]

    arrived = []
    for k in range(min(AHEAD, count)):
        packed = {m: pack(plan, projected, me, k, m) for m in order_of_peers}
        arrived.append(exchange([packed[m] for m in range(1, n)]))

    source = me_scalar ^ jnp.arange(n, dtype=jnp.int32)
    order = (source[:, None] * frames + jnp.arange(frames, dtype=jnp.int32)[None, :]).reshape(-1)
    time_of = jnp.sum(
        jnp.where(order[:, None] == jnp.arange(slots)[None, :], frame_map[None, :], 0), axis=-1
    )
    at_time = time_of[:, None] == jnp.arange(slots, dtype=jnp.int32)[None, :]
    seg_slot = jnp.sum(jnp.where(at_time[None], segments[:, None, :], 0), axis=-1)
    allowed = (time_of[None, :] <= time_of[:, None])[None] & (
        seg_slot[:, None, :] == seg_slot[:, :, None]
    )
    row = jnp.arange(slots * GROUP)
    same_patch = (row[:, None] % GROUP) == (row[None, :] % GROUP)
    wide = jnp.repeat(jnp.repeat(allowed, GROUP, axis=1), GROUP, axis=2)
    bias = jnp.where(wide & same_patch[None], 0.0, -1e30).astype(jnp.float32)

    alone = jnp.sum(allowed.astype(jnp.int32), axis=-1) == 1
    half_of = order // (slots // 2)
    before = (half_of[:, None] == half_of[None, :]) & (order[None, :] < order[:, None])
    rank = jnp.sum((before[None] & ~alone[:, None, :]).astype(jnp.int32), axis=-1)
    here = (half_of == half_of[0])[None]
    kept = jnp.stack(
        [jnp.sum((~alone & here).astype(jnp.int32), -1), jnp.sum((~alone & ~here).astype(jnp.int32), -1)],
        axis=-1,
    )
    tables = [rank.reshape(-1), alone.astype(jnp.int32).reshape(-1), kept.reshape(-1)]

    all_codes = lax.all_gather(codes, "dp", axis=0, tiled=True)
    owned = lax.axis_index("dp") * clips + jnp.arange(clips, dtype=jnp.int32)
    select = (clip_ids[:, None] == owned[None, :]).astype(jnp.float32)
    by_clip = jnp.einsum("ic,ifa->cfa", select, all_codes, precision=HIGHEST)
    codes_slot = jnp.einsum(
        "st,cta->csa", at_time.astype(jnp.float32), by_clip, precision=HIGHEST
    )
    action = jnp.einsum("csa,ad->csd", codes_slot, action_weight, precision=HIGHEST)

    spatial, own = [], []
    for j in range(count):
        for early in plan.chunks[len(spatial) : j + 2]:
            spatial.append(spatial_attention(projected, *early))
        done = temporal_attention(
            plan, projected, arrived[j], bias, action, after(me, *spatial), tables, j
        )
        own.append(done[0])
        outgoing = done[1:]
        if j + 1 == count and n > 2:
            outgoing = lax.optimization_barrier((*outgoing, *arrived[-1][1:]))[: n - 1]
        arrived.append(exchange(outgoing))
    mixed = None
    for j in range(count):
        handed = arrived[j + 2 * AHEAD][0] if plan.slotted(j + AHEAD) else None
        mixed = combine(
            plan, mixed, spatial[j], own[j], arrived[j + AHEAD], handed, projected, action, me, tables,
            j, width,
        )
    return mixed


def solution(mesh):
    return jax.shard_map(
        functools.partial(local, mesh.shape["frame"]),
        mesh=mesh,
        in_specs=(
            P(None, "dp", "frame", None, "mp"),
            P("dp", None, None),
            P(None, "mp"),
            P(),
            P(),
            P("dp", None),
        ),
        out_specs=P("dp", "frame", None, "mp"),
        check_vma=False,
    )
```

```python
import functools
import math

import jax
import jax.numpy as jnp
from jax import lax
from jax.experimental import pallas as pl
from jax.experimental.pallas import tpu as pltpu
from jax.sharding import PartitionSpec as P

E = 128
GROUP = 16
SHARES = (4, 4, 4, 4, 4)
AHEAD = 2
LAST = {1: (2,), 2: (2,), 3: (2, 3)}
EPISODES = 3
HIGHEST = lax.Precision.HIGHEST
VMEM = 48 * 1024 * 1024


def params():
    return pltpu.CompilerParams(vmem_limit_bytes=VMEM)


def pieces(start, heads):
    size = math.gcd(start, heads)
    return heads // size, size, start // size


def spatial_kernel(q_ref, k_ref, v_ref, o_ref):
    heads = q_ref.shape[-1] // E
    for h in range(heads):
        cols = slice(h * E, (h + 1) * E)
        q, k, v = q_ref[0, 0, 0, :, cols], k_ref[0, 0, 0, :, cols], v_ref[0, 0, 0, :, cols]
        s = lax.dot_general(q, k, (((1,), (1,)), ((), ())), preferred_element_type=jnp.float32)
        s = s * (1.0 / E**0.5)
        w = jnp.exp(s - jnp.max(s, axis=-1, keepdims=True))
        p = (w * (1.0 / jnp.sum(w, axis=-1, keepdims=True))).astype(jnp.bfloat16)
        o = jnp.dot(p, v, preferred_element_type=jnp.float32)
        o_ref[0, 0, :, cols] = o.astype(jnp.bfloat16)


def spatial_attention(projected, start, heads):
    _, clips, frames, patches, _ = projected.shape
    count, size, first = pieces(start, heads)
    cols = heads * E
    spec = lambda which: pl.BlockSpec(
        (1, 1, 1, patches, size * E), lambda c, f, i: (which, c, f, 0, first + i)
    )
    return pl.pallas_call(
        spatial_kernel,
        grid=(clips, frames, count),
        in_specs=[spec(0), spec(1), spec(2)],
        out_specs=pl.BlockSpec((1, 1, patches, size * E), lambda c, f, i: (c, f, 0, i)),
        out_shape=jax.ShapeDtypeStruct((clips, frames, patches, cols), jnp.bfloat16),
        compiler_params=params(),
        cost_estimate=pl.CostEstimate(
            flops=4 * clips * frames * patches * patches * cols,
            bytes_accessed=8 * clips * frames * patches * cols,
            transcendentals=clips * frames * patches * patches * (cols // E),
        ),
        name="spatial",
    )(projected, projected, projected)


class Plan:
    def __init__(self, n, frames, patches, heads):
        ends = [round(sum(SHARES[: j + 1]) * heads / sum(SHARES)) for j in range(len(SHARES))]
        self.chunks = [(a, b - a) for a, b in zip([0] + ends, ends) if b > a]
        self.n, self.frames = n, frames
        self.groups = patches // n // GROUP
        alternate = all(a[1] == b[1] for a, b in zip(self.chunks, self.chunks[AHEAD:]))
        self.halved = n == 4 and self.groups == 2 and alternate
        self.slots = n * frames - EPISODES

    def heads(self, j):
        return self.chunks[j][1] if 0 <= j < len(self.chunks) else 0

    def slotted(self, k):
        return self.halved and self.heads(k) > 0 and self.heads(k - AHEAD) > 0

    def parts(self, k, m):
        full = self.groups * self.frames
        sizes = {}
        if self.slotted(k) and m > 1:
            sizes["kv"] = 2 * self.heads(k) * full
            sizes["slots"] = self.heads(k) * self.slots
        else:
            if self.heads(k):
                sizes["qkv"] = 3 * self.heads(k) * full
            if self.heads(k - AHEAD):
                sizes["o"] = self.heads(k - AHEAD) * full
            if m == 1 and self.slotted(k + AHEAD):
                sizes["ql"] = 2 * self.heads(k + AHEAD) * self.frames
            if m == 1 and self.slotted(k - AHEAD):
                sizes["ol"] = 2 * self.heads(k - AHEAD) * self.frames
        at, total = {}, 0
        for name, size in sizes.items():
            at[name] = total
            total += size
        return at, total

    def tile(self, i, g):
        return (i * self.groups + g) * self.frames


def rows_of(g):
    return pl.ds(pl.multiple_of(g * GROUP, GROUP), GROUP)


def head_cols(refs, h):
    size = refs[0].shape[-1] // E
    return refs[h // size], slice(h % size * E, (h % size + 1) * E)


def write_qkv(plan, heads, which, source, out, at):
    for i, a in enumerate(which):
        for h in range(heads):
            x, cut = head_cols(source, h)
            for g in range(plan.groups):
                to = at + plan.tile(i * heads + h, g)
                rows = slice(g * GROUP, (g + 1) * GROUP)
                out[to : to + plan.frames, 0] = x[a, 0, :, rows, cut]


def write_local_queries(plan, heads, parity, sources, out, at):
    for c, source in enumerate(sources):
        for h in range(heads):
            x, cut = head_cols(source, h)
            to = at + (c * heads + h) * plan.frames
            out[to : to + plan.frames, 0] = x[0, 0, :, rows_of(1 - parity), cut]


def pack_kernel(plan, k, m, me_ref, *refs):
    at, _ = plan.parts(k, m)
    count = len(refs) - 1
    blocks = pieces(*plan.chunks[k])[0]
    write_qkv(plan, plan.heads(k), range(3), refs[:blocks], refs[-1], at["qkv"])
    if "ql" in at:
        later = refs[blocks:count]
        half = len(later) // 2
        sources = [later[:half], later[half:]]
        parity = lax.rem(me_ref[0], 2)
        write_local_queries(plan, plan.heads(k + AHEAD), parity, sources, refs[-1], at["ql"])


def peer_rows(plan, chunk, m, arrays, first_array, patches):
    count, size, first = pieces(*chunk)
    return [
        pl.BlockSpec(
            (arrays, 1, plan.frames, patches // plan.n, size * E),
            lambda c, me_ref, *_, i=i: (first_array, c, 0, me_ref[0] ^ m, first + i),
        )
        for i in range(count)
    ]


def tiles(total):
    return pl.BlockSpec((total, 1, GROUP, E), lambda c, *_: (0, c, 0, 0))


def pack(plan, projected, me, k, m):
    _, clips, _, patches, _ = projected.shape
    at, total = plan.parts(k, m)
    specs = peer_rows(plan, plan.chunks[k], m, 3, 1, patches)
    if "ql" in at:
        for peer in (2, 3):
            specs += peer_rows(plan, plan.chunks[k + AHEAD], peer, 1, 3, patches)
    return pl.pallas_call(
        functools.partial(pack_kernel, plan, k, m),
        grid_spec=pltpu.PrefetchScalarGridSpec(
            num_scalar_prefetch=1, grid=(clips,), in_specs=specs, out_specs=tiles(total)
        ),
        out_shape=jax.ShapeDtypeStruct((total, clips, GROUP, E), jnp.bfloat16),
        compiler_params=params(),
        cost_estimate=pl.CostEstimate(
            flops=0, bytes_accessed=4 * total * clips * GROUP * E, transcendentals=0
        ),
        name="pack",
    )(me, *([projected] * len(specs)))


def slot(plan, base, h, i):
    return base + h * plan.slots + jnp.minimum(i, plan.slots - 1)


def temporal_kernel(plan, j, me_ref, rank_ref, alone_ref, kept_ref, *refs):
    n, frames, groups = plan.n, plan.frames, plan.groups
    slots, heads = n * frames, plan.heads(j)
    half = 2 * frames
    c = pl.program_id(0)
    parity = lax.rem(me_ref[0], 2)
    rank = lambda x: rank_ref[c * slots + x]
    alone = lambda x: alone_ref[c * slots + x]
    kept_here, kept_there = kept_ref[c * 2], kept_ref[c * 2 + 1]
    bias_ref, action_ref, refs = refs[0], refs[1], refs[2:]
    bias = bias_ref[0]
    start = plan.chunks[j][0]
    own, refs = refs[: pieces(*plan.chunks[j])[0]], refs[pieces(*plan.chunks[j])[0] :]
    arrived, refs = refs[: n - 1], refs[n - 1 :]
    k = j + AHEAD
    ahead = []
    if plan.heads(k):
        blocks = pieces(*plan.chunks[k])[0]
        for _ in range(1, n):
            ahead.append(refs[:blocks])
            refs = refs[blocks:]
    beyond = []
    if "ql" in plan.parts(k, 1)[0]:
        blocks = pieces(*plan.chunks[k + AHEAD])[0]
        for _ in range(2):
            beyond.append(refs[:blocks])
            refs = refs[blocks:]
    own_out, outs = refs[0], refs[1:]
    came = [plan.parts(j, m)[0] for m in range(1, n)]
    goes = [plan.parts(k, m)[0] for m in range(1, n)]
    slots_in, slots_out = plan.slotted(j), plan.slotted(k)

    for h in range(heads):
        x, cut = head_cols(own, h)
        for r in range(groups):
            g = lax.rem(parity + r, 2) if plan.halved else r
            rows = rows_of(g) if plan.halved else slice(g * GROUP, (g + 1) * GROUP)

            def array(a):
                parts = [x[a, 0, :, rows, cut]]
                for m in range(1, n):
                    at = came[m - 1]
                    if slots_in and m > 1 and a == 0:
                        if m == 2:
                            for y in range(half, slots):
                                to = slot(plan, at["slots"], h, rank(y))
                                parts.append(arrived[1 + r][pl.ds(to, 1), 0])
                        continue
                    i = (a * heads + h) if "qkv" in at else ((a - 1) * heads + h)
                    to = at["qkv" if "qkv" in at else "kv"] + plan.tile(i, g)
                    parts.append(arrived[m - 1][pl.ds(to, frames), 0])
                return jnp.concatenate(parts, axis=0)

            q = array(0).reshape(slots * GROUP, E)
            key = array(1).reshape(slots * GROUP, E)
            action = action_ref[0, :, (start + h) * E : (start + h + 1) * E].reshape(slots, 1, E)
            v = (array(2).astype(jnp.float32) + action).astype(jnp.bfloat16)
            v = v.reshape(slots * GROUP, E)
            s = lax.dot_general(
                q, key, (((1,), (1,)), ((), ())), preferred_element_type=jnp.float32
            )
            s = s * (1.0 / E**0.5) + bias
            w = jnp.exp(s - jnp.max(s, axis=-1, keepdims=True))
            p = (w * (1.0 / jnp.sum(w, axis=-1, keepdims=True))).astype(jnp.bfloat16)
            o = jnp.dot(p, v, preferred_element_type=jnp.float32).astype(jnp.bfloat16)
            o = o.reshape(slots, GROUP, E)
            own_out[pl.ds(plan.tile(h, g), frames), 0] = o[:frames]
            for m in range(1, n):
                if slots_out and m > 1:
                    continue
                to = goes[m - 1]["o"] + plan.tile(h, g)
                outs[m - 1][pl.ds(to, frames), 0] = o[m * frames : (m + 1) * frames]
            if slots_out:
                for y in range(half, slots):

                    @pl.when(alone(y) == 0)
                    def _():
                        to = slot(plan, goes[1]["slots"], h, kept_here + rank(y))
                        outs[1 + r][pl.ds(to, 1), 0] = o[y : y + 1]

    if ahead:
        later = plan.heads(k)
        for m in range(1, n):
            at = goes[m - 1]
            if "qkv" in at:
                write_qkv(plan, later, range(3), ahead[m - 1], outs[m - 1], at["qkv"])
                continue
            write_qkv(plan, later, (1, 2), ahead[m - 1], outs[m - 1], at["kv"])
            for h in range(later):
                x, cut = head_cols(ahead[m - 1], h)
                for y in range(half):
                    local = came[0]["ql"] + ((m ^ 1) - 2) * later * frames + h * frames + y - frames

                    @pl.when(alone(y) == 0)
                    def _():
                        to = slot(plan, at["slots"], h, rank(y))
                        if y < frames:
                            outs[m - 1][pl.ds(to, 1), 0] = x[0, 0, y : y + 1, rows_of(parity), cut]
                        else:
                            outs[m - 1][pl.ds(to, 1), 0] = arrived[0][local : local + 1, 0]

    if beyond:
        write_local_queries(plan, plan.heads(k + AHEAD), parity, beyond, outs[0], goes[0]["ql"])
    if "ol" in goes[0]:
        for i in range(2):
            for h in range(plan.heads(j - AHEAD)):
                for y in range(frames):
                    at = slot(plan, came[1 + i]["slots"], h, kept_there + rank(frames + y))
                    to = goes[0]["ol"] + (i * plan.heads(j - AHEAD) + h) * frames + y
                    outs[0][to : to + 1, 0] = arrived[1 + i][pl.ds(at, 1), 0]


def temporal_attention(plan, projected, arrived, bias, action, me, tables, j):
    _, clips, frames, patches, _ = projected.shape
    n, k, heads = plan.n, j + AHEAD, plan.heads(j)
    slots = n * frames
    own = peer_rows(plan, plan.chunks[j], 0, 3, 1, patches)
    ahead = []
    if plan.heads(k):
        for m in range(1, n):
            ahead += peer_rows(plan, plan.chunks[k], m, 3, 1, patches)
    if "ql" in plan.parts(k, 1)[0]:
        for peer in (2, 3):
            ahead += peer_rows(plan, plan.chunks[k + AHEAD], peer, 1, 3, patches)
    totals = [heads * plan.groups * frames] + [plan.parts(k, m)[1] for m in range(1, n)]
    return pl.pallas_call(
        functools.partial(temporal_kernel, plan, j),
        grid_spec=pltpu.PrefetchScalarGridSpec(
            num_scalar_prefetch=4,
            grid=(clips,),
            in_specs=[
                pl.BlockSpec((1, slots * GROUP, slots * GROUP), lambda c, *_: (c, 0, 0)),
                pl.BlockSpec((1, slots, action.shape[2]), lambda c, *_: (c, 0, 0)),
            ]
            + own
            + [tiles(x.shape[0]) for x in arrived]
            + ahead,
            out_specs=[tiles(total) for total in totals],
        ),
        out_shape=[
            jax.ShapeDtypeStruct((total, clips, GROUP, E), jnp.bfloat16) for total in totals
        ],
        compiler_params=params(),
        cost_estimate=pl.CostEstimate(
            flops=4 * clips * plan.groups * (slots * GROUP) ** 2 * heads * E,
            bytes_accessed=4 * clips * sum(totals) * GROUP * E,
            transcendentals=clips * plan.groups * (slots * GROUP) ** 2 * heads,
        ),
        name="temporal",
    )(
        me,
        *tables,
        bias,
        action,
        *([projected] * len(own)),
        *arrived,
        *([projected] * len(ahead)),
    )


def combine_kernel(plan, j, me_ref, rank_ref, alone_ref, kept_ref, spatial_ref, *refs):
    n, frames, heads = plan.n, plan.frames, plan.heads(j)
    own, back, refs = refs[0], refs[1:n], refs[n:]
    out_ref = refs[-1]
    c = pl.program_id(0)
    me = me_ref[0]
    parity = lax.rem(me, 2)
    slotted = plan.slotted(j + AHEAD)
    came = [plan.parts(j + AHEAD, m)[0] for m in range(1, n)]
    share = plan.groups * GROUP
    kept_there = kept_ref[c * 2 + 1]

    def put(f, i, at, temporal):
        rows = pl.ds(pl.multiple_of(at, GROUP), temporal.shape[-2])
        cut = slice(i * E, (i + 1) * E)
        total = spatial_ref[0, f, rows, cut].astype(jnp.float32) + temporal.astype(jnp.float32)
        out_ref[0, f, rows, cut] = total.astype(jnp.bfloat16)

    blocks, size, _ = pieces(*plan.chunks[j])
    piece = pl.program_id(1)
    for i in range(size):
        h = i if blocks == 1 else piece * size + i
        for m in range(n):
            row = (me ^ m) * share
            if not slotted or m < 2:
                x = own if m == 0 else back[m - 1]
                base = 0 if m == 0 else came[m - 1]["o"]
                for g in range(plan.groups):
                    part = x[pl.ds(base + plan.tile(h, g), frames), 0]
                    put(slice(None), i, row + g * GROUP, part)
                continue
            local = plan.parts(j + 2 * AHEAD, 1)[0]["ol"] + (((m ^ 1) - 2) * heads + h) * frames
            put(slice(None), i, row + (1 - parity) * GROUP, refs[0][pl.ds(local, frames), 0])
            for f in range(frames):
                kept = kept_there + rank_ref[c * n * frames + f]
                to = slot(plan, came[m - 1]["slots"], h, kept)
                put(f, i, row + parity * GROUP, back[m - 1][to, 0])
    if slotted:
        values, action_ref = refs[1], refs[2]
        for f in range(frames):

            @pl.when(alone_ref[c * n * frames + f] == 1)
            def _():
                for i in range(size):
                    cut = slice(i * E, (i + 1) * E)
                    v = values[0, 0, f, :, cut].astype(jnp.float32) + action_ref[0, f : f + 1, cut]
                    put(f, i, 0, v.astype(jnp.bfloat16))


def combine(plan, mixed, spatial, own, back, handed, projected, action, me, tables, j, width):
    clips, frames, patches, cols = spatial.shape
    n = plan.n
    start, heads = plan.chunks[j]
    count, size, first = pieces(start, heads)
    whole = pl.BlockSpec((1, frames, patches, size * E), lambda c, i, *_: (c, 0, 0, i))
    arrays, specs = [spatial, own, *back], [whole] + [tiles(x.shape[0]) for x in (own, *back)]
    if plan.slotted(j + AHEAD):
        arrays += [handed, projected, action]
        specs += [
            tiles(handed.shape[0]),
            pl.BlockSpec(
                (1, 1, frames, patches, size * E), lambda c, i, *_: (5, c, 0, 0, first + i)
            ),
            pl.BlockSpec((1, action.shape[1], size * E), lambda c, i, *_: (c, 0, first + i)),
        ]
    if mixed is not None:
        arrays += [mixed]
        specs += [pl.BlockSpec(memory_space=pl.ANY)]
    return pl.pallas_call(
        functools.partial(combine_kernel, plan, j),
        grid_spec=pltpu.PrefetchScalarGridSpec(
            num_scalar_prefetch=4,
            grid=(clips, count),
            in_specs=specs,
            out_specs=pl.BlockSpec(
                (1, frames, patches, size * E), lambda c, i, *_: (c, 0, 0, first + i)
            ),
        ),
        out_shape=jax.ShapeDtypeStruct((clips, frames, patches, width), jnp.bfloat16),
        input_output_aliases={} if mixed is None else {3 + len(arrays): 0},
        compiler_params=params(),
        cost_estimate=pl.CostEstimate(
            flops=clips * frames * patches * cols,
            bytes_accessed=6 * clips * frames * patches * cols,
            transcendentals=0,
        ),
        name="combine",
    )(me, *tables, *arrays)


def after(x, *others):
    return lax.optimization_barrier((x, *others))[0]


def local(n, projected, codes, action_weight, clip_ids, frame_map, segments):
    _, clips, frames, patches, width = projected.shape
    slots = frame_map.shape[0]
    plan = Plan(n, frames, patches, width // E)
    count = len(plan.chunks)
    me_scalar = lax.axis_index("frame").astype(jnp.int32)
    me = me_scalar[None]
    order_of_peers = [*range(2, n), 1]

    def send(x, m):
        return lax.ppermute(x, "frame", [(i, i ^ m) for i in range(n)])

    def exchange(outgoing):
        got = {m: send(outgoing[m - 1], m) for m in order_of_peers}
        return [got[m] for m in range(1, n)]

    arrived = []
    for k in range(min(AHEAD, count)):
        packed = {m: pack(plan, projected, me, k, m) for m in order_of_peers}
        arrived.append(exchange([packed[m] for m in range(1, n)]))

    source = me_scalar ^ jnp.arange(n, dtype=jnp.int32)
    order = (source[:, None] * frames + jnp.arange(frames, dtype=jnp.int32)[None, :]).reshape(-1)
    time_of = jnp.sum(
        jnp.where(order[:, None] == jnp.arange(slots)[None, :], frame_map[None, :], 0), axis=-1
    )
    at_time = time_of[:, None] == jnp.arange(slots, dtype=jnp.int32)[None, :]
    seg_slot = jnp.sum(jnp.where(at_time[None], segments[:, None, :], 0), axis=-1)
    allowed = (time_of[None, :] <= time_of[:, None])[None] & (
        seg_slot[:, None, :] == seg_slot[:, :, None]
    )
    row = jnp.arange(slots * GROUP)
    same_patch = (row[:, None] % GROUP) == (row[None, :] % GROUP)
    wide = jnp.repeat(jnp.repeat(allowed, GROUP, axis=1), GROUP, axis=2)
    bias = jnp.where(wide & same_patch[None], 0.0, -1e30).astype(jnp.float32)

    alone = jnp.sum(allowed.astype(jnp.int32), axis=-1) == 1
    half_of = order // (slots // 2)
    before = (half_of[:, None] == half_of[None, :]) & (order[None, :] < order[:, None])
    rank = jnp.sum((before[None] & ~alone[:, None, :]).astype(jnp.int32), axis=-1)
    here = (half_of == half_of[0])[None]
    kept = jnp.stack(
        [jnp.sum((~alone & here).astype(jnp.int32), -1), jnp.sum((~alone & ~here).astype(jnp.int32), -1)],
        axis=-1,
    )
    tables = [rank.reshape(-1), alone.astype(jnp.int32).reshape(-1), kept.reshape(-1)]

    all_codes = lax.all_gather(codes, "dp", axis=0, tiled=True)
    owned = lax.axis_index("dp") * clips + jnp.arange(clips, dtype=jnp.int32)
    select = (clip_ids[:, None] == owned[None, :]).astype(jnp.float32)
    by_clip = jnp.einsum("ic,ifa->cfa", select, all_codes, precision=HIGHEST)
    codes_slot = jnp.einsum(
        "st,cta->csa", at_time.astype(jnp.float32), by_clip, precision=HIGHEST
    )
    action = jnp.einsum("csa,ad->csd", codes_slot, action_weight, precision=HIGHEST)

    spatial, own = [], []
    for j in range(count):
        for early in plan.chunks[len(spatial) : j + 2]:
            spatial.append(spatial_attention(projected, *early))
        done = temporal_attention(
            plan, projected, arrived[j], bias, action, after(me, *spatial, *own), tables, j
        )
        own.append(done[0])
        outgoing = done[1:]
        if j + 1 == count and n > max(LAST):
            outgoing = list(outgoing)
            for m, gates in LAST.items():
                outgoing[m - 1] = after(outgoing[m - 1], *[arrived[-1][g - 1] for g in gates])
        arrived.append(exchange(outgoing))
    mixed = None
    for j in range(count):
        handed = arrived[j + 2 * AHEAD][0] if plan.slotted(j + AHEAD) else None
        mixed = combine(
            plan, mixed, spatial[j], own[j], arrived[j + AHEAD], handed, projected, action, me, tables,
            j, width,
        )
    return mixed


def solution(mesh):
    return jax.shard_map(
        functools.partial(local, mesh.shape["frame"]),
        mesh=mesh,
        in_specs=(
            P(None, "dp", "frame", None, "mp"),
            P("dp", None, None),
            P(None, "mp"),
            P(),
            P(),
            P("dp", None),
        ),
        out_specs=P("dp", "frame", None, "mp"),
        check_vma=False,
    )
```

```python
import functools
import math

import jax
import jax.numpy as jnp
from jax import lax
from jax.experimental import pallas as pl
from jax.experimental.pallas import tpu as pltpu
from jax.sharding import PartitionSpec as P

E = 128
GROUP = 16
SHARES = (4, 4, 4, 4, 4)
AHEAD = 2
LATE = (2,)
LAST = {1: (2,), 2: (2,), 3: (2, 3)}
EPISODES = 3
HIGHEST = lax.Precision.HIGHEST
VMEM = 48 * 1024 * 1024


def params():
    return pltpu.CompilerParams(vmem_limit_bytes=VMEM)


def pieces(start, heads):
    size = math.gcd(start, heads)
    return heads // size, size, start // size


def spatial_kernel(q_ref, k_ref, v_ref, o_ref):
    heads = q_ref.shape[-1] // E
    for h in range(heads):
        cols = slice(h * E, (h + 1) * E)
        q, k, v = q_ref[0, 0, 0, :, cols], k_ref[0, 0, 0, :, cols], v_ref[0, 0, 0, :, cols]
        s = lax.dot_general(q, k, (((1,), (1,)), ((), ())), preferred_element_type=jnp.float32)
        s = s * (1.0 / E**0.5)
        w = jnp.exp(s - jnp.max(s, axis=-1, keepdims=True))
        p = (w * (1.0 / jnp.sum(w, axis=-1, keepdims=True))).astype(jnp.bfloat16)
        o = jnp.dot(p, v, preferred_element_type=jnp.float32)
        o_ref[0, 0, :, cols] = o.astype(jnp.bfloat16)


def spatial_attention(projected, start, heads):
    _, clips, frames, patches, _ = projected.shape
    count, size, first = pieces(start, heads)
    cols = heads * E
    spec = lambda which: pl.BlockSpec(
        (1, 1, 1, patches, size * E), lambda c, f, i: (which, c, f, 0, first + i)
    )
    return pl.pallas_call(
        spatial_kernel,
        grid=(clips, frames, count),
        in_specs=[spec(0), spec(1), spec(2)],
        out_specs=pl.BlockSpec((1, 1, patches, size * E), lambda c, f, i: (c, f, 0, i)),
        out_shape=jax.ShapeDtypeStruct((clips, frames, patches, cols), jnp.bfloat16),
        compiler_params=params(),
        cost_estimate=pl.CostEstimate(
            flops=4 * clips * frames * patches * patches * cols,
            bytes_accessed=8 * clips * frames * patches * cols,
            transcendentals=clips * frames * patches * patches * (cols // E),
        ),
        name="spatial",
    )(projected, projected, projected)


class Plan:
    def __init__(self, n, frames, patches, heads):
        ends = [round(sum(SHARES[: j + 1]) * heads / sum(SHARES)) for j in range(len(SHARES))]
        self.chunks = [(a, b - a) for a, b in zip([0] + ends, ends) if b > a]
        self.n, self.frames = n, frames
        self.groups = patches // n // GROUP
        alternate = all(a[1] == b[1] for a, b in zip(self.chunks, self.chunks[AHEAD:]))
        self.halved = n == 4 and self.groups == 2 and alternate
        self.slots = n * frames - EPISODES

    def heads(self, j):
        return self.chunks[j][1] if 0 <= j < len(self.chunks) else 0

    def slotted(self, k):
        return self.halved and self.heads(k) > 0 and self.heads(k - AHEAD) > 0

    def parts(self, k, m):
        full = self.groups * self.frames
        sizes = {}
        if self.slotted(k) and m > 1:
            sizes["slots"] = self.heads(k) * self.slots
            sizes["kv"] = 2 * self.heads(k) * full
        else:
            if self.heads(k - AHEAD):
                sizes["o"] = self.heads(k - AHEAD) * full
            if m == 1 and self.slotted(k - AHEAD):
                sizes["ol"] = 2 * self.heads(k - AHEAD) * self.frames
            if self.heads(k):
                sizes["qkv"] = 3 * self.heads(k) * full
            if m == 1 and self.slotted(k + AHEAD):
                sizes["ql"] = 2 * self.heads(k + AHEAD) * self.frames
        at, total = {}, 0
        for name, size in sizes.items():
            at[name] = total
            total += size
        return at, total

    def results(self, k, m):
        at, total = self.parts(k, m)
        return min([at[x] for x in ("kv", "qkv") if x in at], default=total)

    def tile(self, i, g):
        return (i * self.groups + g) * self.frames


def rows_of(g):
    return pl.ds(pl.multiple_of(g * GROUP, GROUP), GROUP)


def head_cols(refs, h):
    size = refs[0].shape[-1] // E
    return refs[h // size], slice(h % size * E, (h % size + 1) * E)


def write_qkv(plan, heads, which, source, out, at):
    for i, a in enumerate(which):
        for h in range(heads):
            x, cut = head_cols(source, h)
            for g in range(plan.groups):
                to = at + plan.tile(i * heads + h, g)
                rows = slice(g * GROUP, (g + 1) * GROUP)
                out[to : to + plan.frames, 0] = x[a, 0, :, rows, cut]


def write_local_queries(plan, heads, parity, sources, out, at):
    for c, source in enumerate(sources):
        for h in range(heads):
            x, cut = head_cols(source, h)
            to = at + (c * heads + h) * plan.frames
            out[to : to + plan.frames, 0] = x[0, 0, :, rows_of(1 - parity), cut]


def pack_kernel(plan, k, m, me_ref, *refs):
    at, _ = plan.parts(k, m)
    count = len(refs) - 1
    blocks = pieces(*plan.chunks[k])[0]
    write_qkv(plan, plan.heads(k), range(3), refs[:blocks], refs[-1], at["qkv"])
    if "ql" in at:
        later = refs[blocks:count]
        half = len(later) // 2
        sources = [later[:half], later[half:]]
        parity = lax.rem(me_ref[0], 2)
        write_local_queries(plan, plan.heads(k + AHEAD), parity, sources, refs[-1], at["ql"])


def peer_rows(plan, chunk, m, arrays, first_array, patches):
    count, size, first = pieces(*chunk)
    return [
        pl.BlockSpec(
            (arrays, 1, plan.frames, patches // plan.n, size * E),
            lambda c, me_ref, *_, i=i: (first_array, c, 0, me_ref[0] ^ m, first + i),
        )
        for i in range(count)
    ]


def tiles(total):
    return pl.BlockSpec((total, 1, GROUP, E), lambda c, *_: (0, c, 0, 0))


def pack(plan, projected, me, k, m):
    _, clips, _, patches, _ = projected.shape
    at, total = plan.parts(k, m)
    specs = peer_rows(plan, plan.chunks[k], m, 3, 1, patches)
    if "ql" in at:
        for peer in (2, 3):
            specs += peer_rows(plan, plan.chunks[k + AHEAD], peer, 1, 3, patches)
    return pl.pallas_call(
        functools.partial(pack_kernel, plan, k, m),
        grid_spec=pltpu.PrefetchScalarGridSpec(
            num_scalar_prefetch=1, grid=(clips,), in_specs=specs, out_specs=tiles(total)
        ),
        out_shape=jax.ShapeDtypeStruct((total, clips, GROUP, E), jnp.bfloat16),
        compiler_params=params(),
        cost_estimate=pl.CostEstimate(
            flops=0, bytes_accessed=4 * total * clips * GROUP * E, transcendentals=0
        ),
        name="pack",
    )(me, *([projected] * len(specs)))


def slot(plan, base, h, i):
    return base + h * plan.slots + jnp.minimum(i, plan.slots - 1)


def temporal_kernel(plan, j, me_ref, rank_ref, alone_ref, kept_ref, *refs):
    n, frames, groups = plan.n, plan.frames, plan.groups
    slots, heads = n * frames, plan.heads(j)
    half = 2 * frames
    c = pl.program_id(0)
    parity = lax.rem(me_ref[0], 2)
    rank = lambda x: rank_ref[c * slots + x]
    alone = lambda x: alone_ref[c * slots + x]
    kept_here, kept_there = kept_ref[c * 2], kept_ref[c * 2 + 1]
    bias_ref, action_ref, refs = refs[0], refs[1], refs[2:]
    bias = bias_ref[0]
    start = plan.chunks[j][0]
    own, refs = refs[: pieces(*plan.chunks[j])[0]], refs[pieces(*plan.chunks[j])[0] :]
    arrived, refs = refs[: n - 1], refs[n - 1 :]
    k = j + AHEAD
    ahead = []
    if plan.heads(k):
        blocks = pieces(*plan.chunks[k])[0]
        for _ in range(1, n):
            ahead.append(refs[:blocks])
            refs = refs[blocks:]
    beyond = []
    if "ql" in plan.parts(k, 1)[0]:
        blocks = pieces(*plan.chunks[k + AHEAD])[0]
        for _ in range(2):
            beyond.append(refs[:blocks])
            refs = refs[blocks:]
    own_out, outs = refs[0], refs[1:]
    came = [plan.parts(j, m)[0] for m in range(1, n)]
    goes = [plan.parts(k, m)[0] for m in range(1, n)]
    slots_in, slots_out = plan.slotted(j), plan.slotted(k)

    for h in range(heads):
        x, cut = head_cols(own, h)
        for r in range(groups):
            g = lax.rem(parity + r, 2) if plan.halved else r
            rows = rows_of(g) if plan.halved else slice(g * GROUP, (g + 1) * GROUP)

            def array(a):
                parts = [x[a, 0, :, rows, cut]]
                for m in range(1, n):
                    at = came[m - 1]
                    if slots_in and m > 1 and a == 0:
                        if m == 2:
                            for y in range(half, slots):
                                to = slot(plan, at["slots"], h, rank(y))
                                parts.append(arrived[1 + r][pl.ds(to, 1), 0])
                        continue
                    i = (a * heads + h) if "qkv" in at else ((a - 1) * heads + h)
                    to = at["qkv" if "qkv" in at else "kv"] + plan.tile(i, g)
                    parts.append(arrived[m - 1][pl.ds(to, frames), 0])
                return jnp.concatenate(parts, axis=0)

            q = array(0).reshape(slots * GROUP, E)
            key = array(1).reshape(slots * GROUP, E)
            action = action_ref[0, :, (start + h) * E : (start + h + 1) * E].reshape(slots, 1, E)
            v = (array(2).astype(jnp.float32) + action).astype(jnp.bfloat16)
            v = v.reshape(slots * GROUP, E)
            s = lax.dot_general(
                q, key, (((1,), (1,)), ((), ())), preferred_element_type=jnp.float32
            )
            s = s * (1.0 / E**0.5) + bias
            w = jnp.exp(s - jnp.max(s, axis=-1, keepdims=True))
            p = (w * (1.0 / jnp.sum(w, axis=-1, keepdims=True))).astype(jnp.bfloat16)
            o = jnp.dot(p, v, preferred_element_type=jnp.float32).astype(jnp.bfloat16)
            o = o.reshape(slots, GROUP, E)
            own_out[pl.ds(plan.tile(h, g), frames), 0] = o[:frames]
            for m in range(1, n):
                if slots_out and m > 1:
                    continue
                to = goes[m - 1]["o"] + plan.tile(h, g)
                outs[m - 1][pl.ds(to, frames), 0] = o[m * frames : (m + 1) * frames]
            if slots_out:
                for y in range(half, slots):

                    @pl.when(alone(y) == 0)
                    def _():
                        to = slot(plan, goes[1]["slots"], h, kept_here + rank(y))
                        outs[1 + r][pl.ds(to, 1), 0] = o[y : y + 1]

    if ahead:
        later = plan.heads(k)
        for m in range(1, n):
            at = goes[m - 1]
            if "qkv" in at:
                write_qkv(plan, later, range(3), ahead[m - 1], outs[m - 1], at["qkv"])
                continue
            write_qkv(plan, later, (1, 2), ahead[m - 1], outs[m - 1], at["kv"])
            for h in range(later):
                x, cut = head_cols(ahead[m - 1], h)
                for y in range(half):
                    local = came[0]["ql"] + ((m ^ 1) - 2) * later * frames + h * frames + y - frames

                    @pl.when(alone(y) == 0)
                    def _():
                        to = slot(plan, at["slots"], h, rank(y))
                        if y < frames:
                            outs[m - 1][pl.ds(to, 1), 0] = x[0, 0, y : y + 1, rows_of(parity), cut]
                        else:
                            outs[m - 1][pl.ds(to, 1), 0] = arrived[0][local : local + 1, 0]

    if beyond:
        write_local_queries(plan, plan.heads(k + AHEAD), parity, beyond, outs[0], goes[0]["ql"])
    if "ol" in goes[0]:
        for i in range(2):
            for h in range(plan.heads(j - AHEAD)):
                for y in range(frames):
                    at = slot(plan, came[1 + i]["slots"], h, kept_there + rank(frames + y))
                    to = goes[0]["ol"] + (i * plan.heads(j - AHEAD) + h) * frames + y
                    outs[0][to : to + 1, 0] = arrived[1 + i][pl.ds(at, 1), 0]


def temporal_attention(plan, projected, arrived, bias, action, me, tables, j):
    _, clips, frames, patches, _ = projected.shape
    n, k, heads = plan.n, j + AHEAD, plan.heads(j)
    slots = n * frames
    own = peer_rows(plan, plan.chunks[j], 0, 3, 1, patches)
    ahead = []
    if plan.heads(k):
        for m in range(1, n):
            ahead += peer_rows(plan, plan.chunks[k], m, 3, 1, patches)
    if "ql" in plan.parts(k, 1)[0]:
        for peer in (2, 3):
            ahead += peer_rows(plan, plan.chunks[k + AHEAD], peer, 1, 3, patches)
    totals = [heads * plan.groups * frames] + [plan.parts(k, m)[1] for m in range(1, n)]
    return pl.pallas_call(
        functools.partial(temporal_kernel, plan, j),
        grid_spec=pltpu.PrefetchScalarGridSpec(
            num_scalar_prefetch=4,
            grid=(clips,),
            in_specs=[
                pl.BlockSpec((1, slots * GROUP, slots * GROUP), lambda c, *_: (c, 0, 0)),
                pl.BlockSpec((1, slots, action.shape[2]), lambda c, *_: (c, 0, 0)),
            ]
            + own
            + [tiles(x.shape[0]) for x in arrived]
            + ahead,
            out_specs=[tiles(total) for total in totals],
        ),
        out_shape=[
            jax.ShapeDtypeStruct((total, clips, GROUP, E), jnp.bfloat16) for total in totals
        ],
        compiler_params=params(),
        cost_estimate=pl.CostEstimate(
            flops=4 * clips * plan.groups * (slots * GROUP) ** 2 * heads * E,
            bytes_accessed=4 * clips * sum(totals) * GROUP * E,
            transcendentals=clips * plan.groups * (slots * GROUP) ** 2 * heads,
        ),
        name="temporal",
    )(
        me,
        *tables,
        bias,
        action,
        *([projected] * len(own)),
        *arrived,
        *([projected] * len(ahead)),
    )


def combine_kernel(plan, j, me_ref, rank_ref, alone_ref, kept_ref, spatial_ref, *refs):
    n, frames, heads = plan.n, plan.frames, plan.heads(j)
    own, back, refs = refs[0], refs[1:n], refs[n:]
    out_ref = refs[-1]
    c = pl.program_id(0)
    me = me_ref[0]
    parity = lax.rem(me, 2)
    slotted = plan.slotted(j + AHEAD)
    came = [plan.parts(j + AHEAD, m)[0] for m in range(1, n)]
    share = plan.groups * GROUP
    kept_there = kept_ref[c * 2 + 1]

    def put(f, i, at, temporal):
        rows = pl.ds(pl.multiple_of(at, GROUP), temporal.shape[-2])
        cut = slice(i * E, (i + 1) * E)
        total = spatial_ref[0, f, rows, cut].astype(jnp.float32) + temporal.astype(jnp.float32)
        out_ref[0, f, rows, cut] = total.astype(jnp.bfloat16)

    blocks, size, _ = pieces(*plan.chunks[j])
    piece = pl.program_id(1)
    for i in range(size):
        h = i if blocks == 1 else piece * size + i
        for m in range(n):
            row = (me ^ m) * share
            if not slotted or m < 2:
                x = own if m == 0 else back[m - 1]
                base = 0 if m == 0 else came[m - 1]["o"]
                for g in range(plan.groups):
                    part = x[pl.ds(base + plan.tile(h, g), frames), 0]
                    put(slice(None), i, row + g * GROUP, part)
                continue
            local = plan.parts(j + 2 * AHEAD, 1)[0]["ol"] + (((m ^ 1) - 2) * heads + h) * frames
            put(slice(None), i, row + (1 - parity) * GROUP, refs[0][pl.ds(local, frames), 0])
            for f in range(frames):
                kept = kept_there + rank_ref[c * n * frames + f]
                to = slot(plan, came[m - 1]["slots"], h, kept)
                put(f, i, row + parity * GROUP, back[m - 1][to, 0])
    if slotted:
        values, action_ref = refs[1], refs[2]
        for f in range(frames):

            @pl.when(alone_ref[c * n * frames + f] == 1)
            def _():
                for i in range(size):
                    cut = slice(i * E, (i + 1) * E)
                    v = values[0, 0, f, :, cut].astype(jnp.float32) + action_ref[0, f : f + 1, cut]
                    put(f, i, 0, v.astype(jnp.bfloat16))


def combine(plan, mixed, spatial, own, back, handed, projected, action, me, tables, j, width):
    clips, frames, patches, cols = spatial.shape
    n = plan.n
    start, heads = plan.chunks[j]
    count, size, first = pieces(start, heads)
    whole = pl.BlockSpec((1, frames, patches, size * E), lambda c, i, *_: (c, 0, 0, i))
    arrays, specs = [spatial, own, *back], [whole, tiles(own.shape[0])]
    specs += [tiles(plan.results(j + AHEAD, m)) for m in range(1, n)]
    if plan.slotted(j + AHEAD):
        arrays += [handed, projected, action]
        specs += [
            tiles(plan.results(j + 2 * AHEAD, 1)),
            pl.BlockSpec(
                (1, 1, frames, patches, size * E), lambda c, i, *_: (5, c, 0, 0, first + i)
            ),
            pl.BlockSpec((1, action.shape[1], size * E), lambda c, i, *_: (c, 0, first + i)),
        ]
    if mixed is not None:
        arrays += [mixed]
        specs += [pl.BlockSpec(memory_space=pl.ANY)]
    return pl.pallas_call(
        functools.partial(combine_kernel, plan, j),
        grid_spec=pltpu.PrefetchScalarGridSpec(
            num_scalar_prefetch=4,
            grid=(clips, count),
            in_specs=specs,
            out_specs=pl.BlockSpec(
                (1, frames, patches, size * E), lambda c, i, *_: (c, 0, 0, first + i)
            ),
        ),
        out_shape=jax.ShapeDtypeStruct((clips, frames, patches, width), jnp.bfloat16),
        input_output_aliases={} if mixed is None else {3 + len(arrays): 0},
        compiler_params=params(),
        cost_estimate=pl.CostEstimate(
            flops=clips * frames * patches * cols,
            bytes_accessed=6 * clips * frames * patches * cols,
            transcendentals=0,
        ),
        name="combine",
    )(me, *tables, *arrays)


def add_rows_kernel(plan, heads, base, me_ref, spatial_ref, part_ref, *refs):
    out_ref = refs[-1]
    for h in range(heads):
        cut = slice(h * E, (h + 1) * E)
        for g in range(plan.groups):
            rows = slice(g * GROUP, (g + 1) * GROUP)
            to = base + plan.tile(h, g)
            one, other = spatial_ref[0, :, rows, cut], part_ref[to : to + plan.frames, 0]
            total = one.astype(jnp.float32) + other.astype(jnp.float32)
            out_ref[0, :, rows, cut] = total.astype(jnp.bfloat16)


def add_rows(plan, mixed, spatial, part, me, j, m):
    clips, frames, patches, cols = spatial.shape
    start, heads = plan.chunks[j]
    rows = patches // plan.n
    base = plan.parts(j + AHEAD, m)[0]["o"] if m else 0
    held = base + heads * plan.groups * frames
    return pl.pallas_call(
        functools.partial(add_rows_kernel, plan, heads, base),
        grid_spec=pltpu.PrefetchScalarGridSpec(
            num_scalar_prefetch=1,
            grid=(clips,),
            in_specs=[
                pl.BlockSpec((1, frames, rows, cols), lambda c, me_ref: (c, 0, me_ref[0] ^ m, 0)),
                tiles(held),
                pl.BlockSpec(memory_space=pl.ANY),
            ],
            out_specs=pl.BlockSpec(
                (1, frames, rows, cols),
                lambda c, me_ref: (c, 0, me_ref[0] ^ m, start // heads),
            ),
        ),
        out_shape=jax.ShapeDtypeStruct(mixed.shape, mixed.dtype),
        input_output_aliases={3: 0},
        compiler_params=params(),
        cost_estimate=pl.CostEstimate(
            flops=clips * frames * rows * cols,
            bytes_accessed=6 * clips * frames * rows * cols,
            transcendentals=0,
        ),
        name="add_rows",
    )(me, spatial, part, mixed)


def after(x, *others):
    return lax.optimization_barrier((x, *others))[0]


def local(n, projected, codes, action_weight, clip_ids, frame_map, segments):
    _, clips, frames, patches, width = projected.shape
    slots = frame_map.shape[0]
    plan = Plan(n, frames, patches, width // E)
    count = len(plan.chunks)
    me_scalar = lax.axis_index("frame").astype(jnp.int32)
    me = me_scalar[None]
    order_of_peers = [*range(2, n), 1]

    def send(x, m):
        return lax.ppermute(x, "frame", [(i, i ^ m) for i in range(n)])

    def exchange(outgoing):
        got = {m: send(outgoing[m - 1], m) for m in order_of_peers}
        return [got[m] for m in range(1, n)]

    arrived = []
    for k in range(min(AHEAD, count)):
        packed = {m: pack(plan, projected, me, k, m) for m in order_of_peers}
        arrived.append(exchange([packed[m] for m in range(1, n)]))

    source = me_scalar ^ jnp.arange(n, dtype=jnp.int32)
    order = (source[:, None] * frames + jnp.arange(frames, dtype=jnp.int32)[None, :]).reshape(-1)
    time_of = jnp.sum(
        jnp.where(order[:, None] == jnp.arange(slots)[None, :], frame_map[None, :], 0), axis=-1
    )
    at_time = time_of[:, None] == jnp.arange(slots, dtype=jnp.int32)[None, :]
    seg_slot = jnp.sum(jnp.where(at_time[None], segments[:, None, :], 0), axis=-1)
    allowed = (time_of[None, :] <= time_of[:, None])[None] & (
        seg_slot[:, None, :] == seg_slot[:, :, None]
    )
    row = jnp.arange(slots * GROUP)
    same_patch = (row[:, None] % GROUP) == (row[None, :] % GROUP)
    wide = jnp.repeat(jnp.repeat(allowed, GROUP, axis=1), GROUP, axis=2)
    bias = jnp.where(wide & same_patch[None], 0.0, -1e30).astype(jnp.float32)

    alone = jnp.sum(allowed.astype(jnp.int32), axis=-1) == 1
    half_of = order // (slots // 2)
    before = (half_of[:, None] == half_of[None, :]) & (order[None, :] < order[:, None])
    rank = jnp.sum((before[None] & ~alone[:, None, :]).astype(jnp.int32), axis=-1)
    here = (half_of == half_of[0])[None]
    kept = jnp.stack(
        [jnp.sum((~alone & here).astype(jnp.int32), -1), jnp.sum((~alone & ~here).astype(jnp.int32), -1)],
        axis=-1,
    )
    tables = [rank.reshape(-1), alone.astype(jnp.int32).reshape(-1), kept.reshape(-1)]

    all_codes = lax.all_gather(codes, "dp", axis=0, tiled=True)
    owned = lax.axis_index("dp") * clips + jnp.arange(clips, dtype=jnp.int32)
    select = (clip_ids[:, None] == owned[None, :]).astype(jnp.float32)
    by_clip = jnp.einsum("ic,ifa->cfa", select, all_codes, precision=HIGHEST)
    codes_slot = jnp.einsum(
        "st,cta->csa", at_time.astype(jnp.float32), by_clip, precision=HIGHEST
    )
    action = jnp.einsum("csa,ad->csd", codes_slot, action_weight, precision=HIGHEST)

    spatial, own, mixed = [], [], None

    def add(mixed, j, late=()):
        back = [own[j] if m in late else arrived[j + AHEAD][m - 1] for m in range(1, n)]
        handed = arrived[j + 2 * AHEAD][0] if plan.slotted(j + AHEAD) else None
        return combine(
            plan, mixed, spatial[j], own[j], back, handed, projected, action, me, tables,
            j, width,
        )

    for j in range(count):
        for early in plan.chunks[len(spatial) : j + 2]:
            spatial.append(spatial_attention(projected, *early))
        ready = [*spatial, *own]
        done = temporal_attention(
            plan, projected, arrived[j], bias, action, after(me, *ready), tables, j
        )
        own.append(done[0])
        outgoing = done[1:]
        if j + 1 == count and n > max(LAST):
            outgoing = list(outgoing)
            for m, gates in LAST.items():
                outgoing[m - 1] = after(outgoing[m - 1], *[arrived[-1][g - 1] for g in gates])
        arrived.append(exchange(outgoing))
    last = count - 1
    start, heads = plan.chunks[last]
    split = n > max(LATE) and not plan.slotted(last + AHEAD) and start % heads == 0
    for j in range(count):
        mixed = add(mixed, j, LATE if split and j == last else ())
    if split:
        for m in LATE:
            mixed = add_rows(plan, mixed, spatial[last], arrived[last + AHEAD][m - 1], me, last, m)
    return mixed


def solution(mesh):
    return jax.shard_map(
        functools.partial(local, mesh.shape["frame"]),
        mesh=mesh,
        in_specs=(
            P(None, "dp", "frame", None, "mp"),
            P("dp", None, None),
            P(None, "mp"),
            P(),
            P(),
            P("dp", None),
        ),
        out_specs=P("dp", "frame", None, "mp"),
        check_vma=False,
    )
```

```python
import functools
import math

import jax
import jax.numpy as jnp
from jax import lax
from jax.experimental import pallas as pl
from jax.experimental.pallas import tpu as pltpu
from jax.sharding import PartitionSpec as P

E = 128
GROUP = 16
SHARES = (4, 4, 4, 4, 4)
AHEAD = 2
LATE = (2,)
LAST = {1: (2,), 3: (2, 3)}
EPISODES = 3
HIGHEST = lax.Precision.HIGHEST
VMEM = 48 * 1024 * 1024


def params():
    return pltpu.CompilerParams(vmem_limit_bytes=VMEM)


def pieces(start, heads):
    size = math.gcd(start, heads)
    return heads // size, size, start // size


def spatial_kernel(q_ref, k_ref, v_ref, o_ref):
    heads = q_ref.shape[-1] // E
    for h in range(heads):
        cols = slice(h * E, (h + 1) * E)
        q, k, v = q_ref[0, 0, 0, :, cols], k_ref[0, 0, 0, :, cols], v_ref[0, 0, 0, :, cols]
        s = lax.dot_general(q, k, (((1,), (1,)), ((), ())), preferred_element_type=jnp.float32)
        s = s * (1.0 / E**0.5)
        w = jnp.exp(s - jnp.max(s, axis=-1, keepdims=True))
        p = (w * (1.0 / jnp.sum(w, axis=-1, keepdims=True))).astype(jnp.bfloat16)
        o = jnp.dot(p, v, preferred_element_type=jnp.float32)
        o_ref[0, 0, :, cols] = o.astype(jnp.bfloat16)


def spatial_attention(projected, start, heads):
    _, clips, frames, patches, _ = projected.shape
    count, size, first = pieces(start, heads)
    cols = heads * E
    spec = lambda which: pl.BlockSpec(
        (1, 1, 1, patches, size * E), lambda c, f, i: (which, c, f, 0, first + i)
    )
    return pl.pallas_call(
        spatial_kernel,
        grid=(clips, frames, count),
        in_specs=[spec(0), spec(1), spec(2)],
        out_specs=pl.BlockSpec((1, 1, patches, size * E), lambda c, f, i: (c, f, 0, i)),
        out_shape=jax.ShapeDtypeStruct((clips, frames, patches, cols), jnp.bfloat16),
        compiler_params=params(),
        cost_estimate=pl.CostEstimate(
            flops=4 * clips * frames * patches * patches * cols,
            bytes_accessed=8 * clips * frames * patches * cols,
            transcendentals=clips * frames * patches * patches * (cols // E),
        ),
        name="spatial",
    )(projected, projected, projected)


class Plan:
    def __init__(self, n, frames, patches, heads):
        ends = [round(sum(SHARES[: j + 1]) * heads / sum(SHARES)) for j in range(len(SHARES))]
        self.chunks = [(a, b - a) for a, b in zip([0] + ends, ends) if b > a]
        self.n, self.frames = n, frames
        self.groups = patches // n // GROUP
        alternate = all(a[1] == b[1] for a, b in zip(self.chunks, self.chunks[AHEAD:]))
        self.halved = n == 4 and self.groups == 2 and alternate
        self.slots = n * frames - EPISODES

    def heads(self, j):
        return self.chunks[j][1] if 0 <= j < len(self.chunks) else 0

    def slotted(self, k):
        return self.halved and self.heads(k) > 0 and self.heads(k - AHEAD) > 0

    def parts(self, k, m):
        full = self.groups * self.frames
        sizes = {}
        if self.slotted(k) and m > 1:
            sizes["slots"] = self.heads(k) * self.slots
            sizes["kv"] = 2 * self.heads(k) * full
        else:
            if self.heads(k - AHEAD):
                sizes["o"] = self.heads(k - AHEAD) * full
            if m == 1 and self.slotted(k - AHEAD):
                sizes["ol"] = 2 * self.heads(k - AHEAD) * self.frames
            if self.heads(k):
                sizes["qkv"] = 3 * self.heads(k) * full
            if m == 1 and self.slotted(k + AHEAD):
                sizes["ql"] = 2 * self.heads(k + AHEAD) * self.frames
        at, total = {}, 0
        for name, size in sizes.items():
            at[name] = total
            total += size
        return at, total

    def results(self, k, m):
        at, total = self.parts(k, m)
        return min([at[x] for x in ("kv", "qkv") if x in at], default=total)

    def tile(self, i, g):
        return (i * self.groups + g) * self.frames


def rows_of(g):
    return pl.ds(pl.multiple_of(g * GROUP, GROUP), GROUP)


def head_cols(refs, h):
    size = refs[0].shape[-1] // E
    return refs[h // size], slice(h % size * E, (h % size + 1) * E)


def write_qkv(plan, heads, which, source, out, at):
    for i, a in enumerate(which):
        for h in range(heads):
            x, cut = head_cols(source, h)
            for g in range(plan.groups):
                to = at + plan.tile(i * heads + h, g)
                rows = slice(g * GROUP, (g + 1) * GROUP)
                out[to : to + plan.frames, 0] = x[a, 0, :, rows, cut]


def write_local_queries(plan, heads, parity, sources, out, at):
    for c, source in enumerate(sources):
        for h in range(heads):
            x, cut = head_cols(source, h)
            to = at + (c * heads + h) * plan.frames
            out[to : to + plan.frames, 0] = x[0, 0, :, rows_of(1 - parity), cut]


def pack_kernel(plan, k, m, me_ref, *refs):
    at, _ = plan.parts(k, m)
    count = len(refs) - 1
    blocks = pieces(*plan.chunks[k])[0]
    write_qkv(plan, plan.heads(k), range(3), refs[:blocks], refs[-1], at["qkv"])
    if "ql" in at:
        later = refs[blocks:count]
        half = len(later) // 2
        sources = [later[:half], later[half:]]
        parity = lax.rem(me_ref[0], 2)
        write_local_queries(plan, plan.heads(k + AHEAD), parity, sources, refs[-1], at["ql"])


def peer_rows(plan, chunk, m, arrays, first_array, patches):
    count, size, first = pieces(*chunk)
    return [
        pl.BlockSpec(
            (arrays, 1, plan.frames, patches // plan.n, size * E),
            lambda c, me_ref, *_, i=i: (first_array, c, 0, me_ref[0] ^ m, first + i),
        )
        for i in range(count)
    ]


def tiles(total):
    return pl.BlockSpec((total, 1, GROUP, E), lambda c, *_: (0, c, 0, 0))


def pack(plan, projected, me, k, m):
    _, clips, _, patches, _ = projected.shape
    at, total = plan.parts(k, m)
    specs = peer_rows(plan, plan.chunks[k], m, 3, 1, patches)
    if "ql" in at:
        for peer in (2, 3):
            specs += peer_rows(plan, plan.chunks[k + AHEAD], peer, 1, 3, patches)
    return pl.pallas_call(
        functools.partial(pack_kernel, plan, k, m),
        grid_spec=pltpu.PrefetchScalarGridSpec(
            num_scalar_prefetch=1, grid=(clips,), in_specs=specs, out_specs=tiles(total)
        ),
        out_shape=jax.ShapeDtypeStruct((total, clips, GROUP, E), jnp.bfloat16),
        compiler_params=params(),
        cost_estimate=pl.CostEstimate(
            flops=0, bytes_accessed=4 * total * clips * GROUP * E, transcendentals=0
        ),
        name="pack",
    )(me, *([projected] * len(specs)))


def slot(plan, base, h, i):
    return base + h * plan.slots + jnp.minimum(i, plan.slots - 1)


def temporal_kernel(plan, j, me_ref, rank_ref, alone_ref, kept_ref, *refs):
    n, frames, groups = plan.n, plan.frames, plan.groups
    slots, heads = n * frames, plan.heads(j)
    half = 2 * frames
    c = pl.program_id(0)
    parity = lax.rem(me_ref[0], 2)
    rank = lambda x: rank_ref[c * slots + x]
    alone = lambda x: alone_ref[c * slots + x]
    kept_here, kept_there = kept_ref[c * 2], kept_ref[c * 2 + 1]
    bias_ref, action_ref, refs = refs[0], refs[1], refs[2:]
    bias = bias_ref[0]
    start = plan.chunks[j][0]
    own, refs = refs[: pieces(*plan.chunks[j])[0]], refs[pieces(*plan.chunks[j])[0] :]
    arrived, refs = refs[: n - 1], refs[n - 1 :]
    k = j + AHEAD
    ahead = []
    if plan.heads(k):
        blocks = pieces(*plan.chunks[k])[0]
        for _ in range(1, n):
            ahead.append(refs[:blocks])
            refs = refs[blocks:]
    beyond = []
    if "ql" in plan.parts(k, 1)[0]:
        blocks = pieces(*plan.chunks[k + AHEAD])[0]
        for _ in range(2):
            beyond.append(refs[:blocks])
            refs = refs[blocks:]
    own_out, outs = refs[0], refs[1:]
    came = [plan.parts(j, m)[0] for m in range(1, n)]
    goes = [plan.parts(k, m)[0] for m in range(1, n)]
    slots_in, slots_out = plan.slotted(j), plan.slotted(k)

    for h in range(heads):
        x, cut = head_cols(own, h)
        for r in range(groups):
            g = lax.rem(parity + r, 2) if plan.halved else r
            rows = rows_of(g) if plan.halved else slice(g * GROUP, (g + 1) * GROUP)

            def array(a):
                parts = [x[a, 0, :, rows, cut]]
                for m in range(1, n):
                    at = came[m - 1]
                    if slots_in and m > 1 and a == 0:
                        if m == 2:
                            for y in range(half, slots):
                                to = slot(plan, at["slots"], h, rank(y))
                                parts.append(arrived[1 + r][pl.ds(to, 1), 0])
                        continue
                    i = (a * heads + h) if "qkv" in at else ((a - 1) * heads + h)
                    to = at["qkv" if "qkv" in at else "kv"] + plan.tile(i, g)
                    parts.append(arrived[m - 1][pl.ds(to, frames), 0])
                return jnp.concatenate(parts, axis=0)

            q = array(0).reshape(slots * GROUP, E)
            key = array(1).reshape(slots * GROUP, E)
            action = action_ref[0, :, (start + h) * E : (start + h + 1) * E].reshape(slots, 1, E)
            v = (array(2).astype(jnp.float32) + action).astype(jnp.bfloat16)
            v = v.reshape(slots * GROUP, E)
            s = lax.dot_general(
                q, key, (((1,), (1,)), ((), ())), preferred_element_type=jnp.float32
            )
            s = s * (1.0 / E**0.5) + bias
            w = jnp.exp(s - jnp.max(s, axis=-1, keepdims=True))
            p = (w * (1.0 / jnp.sum(w, axis=-1, keepdims=True))).astype(jnp.bfloat16)
            o = jnp.dot(p, v, preferred_element_type=jnp.float32).astype(jnp.bfloat16)
            o = o.reshape(slots, GROUP, E)
            own_out[pl.ds(plan.tile(h, g), frames), 0] = o[:frames]
            for m in range(1, n):
                if slots_out and m > 1:
                    continue
                to = goes[m - 1]["o"] + plan.tile(h, g)
                outs[m - 1][pl.ds(to, frames), 0] = o[m * frames : (m + 1) * frames]
            if slots_out:
                for y in range(half, slots):

                    @pl.when(alone(y) == 0)
                    def _():
                        to = slot(plan, goes[1]["slots"], h, kept_here + rank(y))
                        outs[1 + r][pl.ds(to, 1), 0] = o[y : y + 1]

    if ahead:
        later = plan.heads(k)
        for m in range(1, n):
            at = goes[m - 1]
            if "qkv" in at:
                write_qkv(plan, later, range(3), ahead[m - 1], outs[m - 1], at["qkv"])
                continue
            write_qkv(plan, later, (1, 2), ahead[m - 1], outs[m - 1], at["kv"])
            for h in range(later):
                x, cut = head_cols(ahead[m - 1], h)
                for y in range(half):
                    local = came[0]["ql"] + ((m ^ 1) - 2) * later * frames + h * frames + y - frames

                    @pl.when(alone(y) == 0)
                    def _():
                        to = slot(plan, at["slots"], h, rank(y))
                        if y < frames:
                            outs[m - 1][pl.ds(to, 1), 0] = x[0, 0, y : y + 1, rows_of(parity), cut]
                        else:
                            outs[m - 1][pl.ds(to, 1), 0] = arrived[0][local : local + 1, 0]

    if beyond:
        write_local_queries(plan, plan.heads(k + AHEAD), parity, beyond, outs[0], goes[0]["ql"])
    if "ol" in goes[0]:
        for i in range(2):
            for h in range(plan.heads(j - AHEAD)):
                for y in range(frames):
                    at = slot(plan, came[1 + i]["slots"], h, kept_there + rank(frames + y))
                    to = goes[0]["ol"] + (i * plan.heads(j - AHEAD) + h) * frames + y
                    outs[0][to : to + 1, 0] = arrived[1 + i][pl.ds(at, 1), 0]


def temporal_attention(plan, projected, arrived, bias, action, me, tables, j):
    _, clips, frames, patches, _ = projected.shape
    n, k, heads = plan.n, j + AHEAD, plan.heads(j)
    slots = n * frames
    own = peer_rows(plan, plan.chunks[j], 0, 3, 1, patches)
    ahead = []
    if plan.heads(k):
        for m in range(1, n):
            ahead += peer_rows(plan, plan.chunks[k], m, 3, 1, patches)
    if "ql" in plan.parts(k, 1)[0]:
        for peer in (2, 3):
            ahead += peer_rows(plan, plan.chunks[k + AHEAD], peer, 1, 3, patches)
    totals = [heads * plan.groups * frames] + [plan.parts(k, m)[1] for m in range(1, n)]
    return pl.pallas_call(
        functools.partial(temporal_kernel, plan, j),
        grid_spec=pltpu.PrefetchScalarGridSpec(
            num_scalar_prefetch=4,
            grid=(clips,),
            in_specs=[
                pl.BlockSpec((1, slots * GROUP, slots * GROUP), lambda c, *_: (c, 0, 0)),
                pl.BlockSpec((1, slots, action.shape[2]), lambda c, *_: (c, 0, 0)),
            ]
            + own
            + [tiles(x.shape[0]) for x in arrived]
            + ahead,
            out_specs=[tiles(total) for total in totals],
        ),
        out_shape=[
            jax.ShapeDtypeStruct((total, clips, GROUP, E), jnp.bfloat16) for total in totals
        ],
        compiler_params=params(),
        cost_estimate=pl.CostEstimate(
            flops=4 * clips * plan.groups * (slots * GROUP) ** 2 * heads * E,
            bytes_accessed=4 * clips * sum(totals) * GROUP * E,
            transcendentals=clips * plan.groups * (slots * GROUP) ** 2 * heads,
        ),
        name="temporal",
    )(
        me,
        *tables,
        bias,
        action,
        *([projected] * len(own)),
        *arrived,
        *([projected] * len(ahead)),
    )


def combine_kernel(plan, j, me_ref, rank_ref, alone_ref, kept_ref, spatial_ref, *refs):
    n, frames, heads = plan.n, plan.frames, plan.heads(j)
    own, back, refs = refs[0], refs[1:n], refs[n:]
    out_ref = refs[-1]
    c = pl.program_id(0)
    me = me_ref[0]
    parity = lax.rem(me, 2)
    slotted = plan.slotted(j + AHEAD)
    came = [plan.parts(j + AHEAD, m)[0] for m in range(1, n)]
    share = plan.groups * GROUP
    kept_there = kept_ref[c * 2 + 1]

    def put(f, i, at, temporal):
        rows = pl.ds(pl.multiple_of(at, GROUP), temporal.shape[-2])
        cut = slice(i * E, (i + 1) * E)
        total = spatial_ref[0, f, rows, cut].astype(jnp.float32) + temporal.astype(jnp.float32)
        out_ref[0, f, rows, cut] = total.astype(jnp.bfloat16)

    blocks, size, _ = pieces(*plan.chunks[j])
    piece = pl.program_id(1)
    for i in range(size):
        h = i if blocks == 1 else piece * size + i
        for m in range(n):
            row = (me ^ m) * share
            if not slotted or m < 2:
                x = own if m == 0 else back[m - 1]
                base = 0 if m == 0 else came[m - 1]["o"]
                for g in range(plan.groups):
                    part = x[pl.ds(base + plan.tile(h, g), frames), 0]
                    put(slice(None), i, row + g * GROUP, part)
                continue
            local = plan.parts(j + 2 * AHEAD, 1)[0]["ol"] + (((m ^ 1) - 2) * heads + h) * frames
            put(slice(None), i, row + (1 - parity) * GROUP, refs[0][pl.ds(local, frames), 0])
            for f in range(frames):
                kept = kept_there + rank_ref[c * n * frames + f]
                to = slot(plan, came[m - 1]["slots"], h, kept)
                put(f, i, row + parity * GROUP, back[m - 1][to, 0])
    if slotted:
        values, action_ref = refs[1], refs[2]
        for f in range(frames):

            @pl.when(alone_ref[c * n * frames + f] == 1)
            def _():
                for i in range(size):
                    cut = slice(i * E, (i + 1) * E)
                    v = values[0, 0, f, :, cut].astype(jnp.float32) + action_ref[0, f : f + 1, cut]
                    put(f, i, 0, v.astype(jnp.bfloat16))


def combine(plan, mixed, spatial, own, back, handed, projected, action, me, tables, j, width):
    clips, frames, patches, cols = spatial.shape
    n = plan.n
    start, heads = plan.chunks[j]
    count, size, first = pieces(start, heads)
    whole = pl.BlockSpec((1, frames, patches, size * E), lambda c, i, *_: (c, 0, 0, i))
    arrays, specs = [spatial, own, *back], [whole, tiles(own.shape[0])]
    specs += [tiles(plan.results(j + AHEAD, m)) for m in range(1, n)]
    if plan.slotted(j + AHEAD):
        arrays += [handed, projected, action]
        specs += [
            tiles(plan.results(j + 2 * AHEAD, 1)),
            pl.BlockSpec(
                (1, 1, frames, patches, size * E), lambda c, i, *_: (5, c, 0, 0, first + i)
            ),
            pl.BlockSpec((1, action.shape[1], size * E), lambda c, i, *_: (c, 0, first + i)),
        ]
    if mixed is not None:
        arrays += [mixed]
        specs += [pl.BlockSpec(memory_space=pl.ANY)]
    return pl.pallas_call(
        functools.partial(combine_kernel, plan, j),
        grid_spec=pltpu.PrefetchScalarGridSpec(
            num_scalar_prefetch=4,
            grid=(clips, count),
            in_specs=specs,
            out_specs=pl.BlockSpec(
                (1, frames, patches, size * E), lambda c, i, *_: (c, 0, 0, first + i)
            ),
        ),
        out_shape=jax.ShapeDtypeStruct((clips, frames, patches, width), jnp.bfloat16),
        input_output_aliases={} if mixed is None else {3 + len(arrays): 0},
        compiler_params=params(),
        cost_estimate=pl.CostEstimate(
            flops=clips * frames * patches * cols,
            bytes_accessed=6 * clips * frames * patches * cols,
            transcendentals=0,
        ),
        name="combine",
    )(me, *tables, *arrays)


def add_rows_kernel(plan, heads, base, me_ref, spatial_ref, part_ref, *refs):
    out_ref = refs[-1]
    for h in range(heads):
        cut = slice(h * E, (h + 1) * E)
        for g in range(plan.groups):
            rows = slice(g * GROUP, (g + 1) * GROUP)
            to = base + plan.tile(h, g)
            one, other = spatial_ref[0, :, rows, cut], part_ref[to : to + plan.frames, 0]
            total = one.astype(jnp.float32) + other.astype(jnp.float32)
            out_ref[0, :, rows, cut] = total.astype(jnp.bfloat16)


def add_rows(plan, mixed, spatial, part, me, j, m):
    clips, frames, patches, cols = spatial.shape
    start, heads = plan.chunks[j]
    rows = patches // plan.n
    base = plan.parts(j + AHEAD, m)[0]["o"] if m else 0
    held = base + heads * plan.groups * frames
    return pl.pallas_call(
        functools.partial(add_rows_kernel, plan, heads, base),
        grid_spec=pltpu.PrefetchScalarGridSpec(
            num_scalar_prefetch=1,
            grid=(clips,),
            in_specs=[
                pl.BlockSpec((1, frames, rows, cols), lambda c, me_ref: (c, 0, me_ref[0] ^ m, 0)),
                tiles(held),
                pl.BlockSpec(memory_space=pl.ANY),
            ],
            out_specs=pl.BlockSpec(
                (1, frames, rows, cols),
                lambda c, me_ref: (c, 0, me_ref[0] ^ m, start // heads),
            ),
        ),
        out_shape=jax.ShapeDtypeStruct(mixed.shape, mixed.dtype),
        input_output_aliases={3: 0},
        compiler_params=params(),
        cost_estimate=pl.CostEstimate(
            flops=clips * frames * rows * cols,
            bytes_accessed=6 * clips * frames * rows * cols,
            transcendentals=0,
        ),
        name="add_rows",
    )(me, spatial, part, mixed)


def after(x, *others):
    return lax.optimization_barrier((x, *others))[0]


def local(n, projected, codes, action_weight, clip_ids, frame_map, segments):
    _, clips, frames, patches, width = projected.shape
    slots = frame_map.shape[0]
    plan = Plan(n, frames, patches, width // E)
    count = len(plan.chunks)
    me_scalar = lax.axis_index("frame").astype(jnp.int32)
    me = me_scalar[None]
    order_of_peers = [*range(2, n), 1]

    def send(x, m):
        return lax.ppermute(x, "frame", [(i, i ^ m) for i in range(n)])

    def exchange(outgoing):
        got = {m: send(outgoing[m - 1], m) for m in order_of_peers}
        return [got[m] for m in range(1, n)]

    arrived = []
    for k in range(min(AHEAD, count)):
        packed = {m: pack(plan, projected, me, k, m) for m in order_of_peers}
        arrived.append(exchange([packed[m] for m in range(1, n)]))

    source = me_scalar ^ jnp.arange(n, dtype=jnp.int32)
    order = (source[:, None] * frames + jnp.arange(frames, dtype=jnp.int32)[None, :]).reshape(-1)
    time_of = jnp.sum(
        jnp.where(order[:, None] == jnp.arange(slots)[None, :], frame_map[None, :], 0), axis=-1
    )
    at_time = time_of[:, None] == jnp.arange(slots, dtype=jnp.int32)[None, :]
    seg_slot = jnp.sum(jnp.where(at_time[None], segments[:, None, :], 0), axis=-1)
    allowed = (time_of[None, :] <= time_of[:, None])[None] & (
        seg_slot[:, None, :] == seg_slot[:, :, None]
    )
    row = jnp.arange(slots * GROUP)
    same_patch = (row[:, None] % GROUP) == (row[None, :] % GROUP)
    wide = jnp.repeat(jnp.repeat(allowed, GROUP, axis=1), GROUP, axis=2)
    bias = jnp.where(wide & same_patch[None], 0.0, -1e30).astype(jnp.float32)

    alone = jnp.sum(allowed.astype(jnp.int32), axis=-1) == 1
    half_of = order // (slots // 2)
    before = (half_of[:, None] == half_of[None, :]) & (order[None, :] < order[:, None])
    rank = jnp.sum((before[None] & ~alone[:, None, :]).astype(jnp.int32), axis=-1)
    here = (half_of == half_of[0])[None]
    kept = jnp.stack(
        [jnp.sum((~alone & here).astype(jnp.int32), -1), jnp.sum((~alone & ~here).astype(jnp.int32), -1)],
        axis=-1,
    )
    tables = [rank.reshape(-1), alone.astype(jnp.int32).reshape(-1), kept.reshape(-1)]

    all_codes = lax.all_gather(codes, "dp", axis=0, tiled=True)
    owned = lax.axis_index("dp") * clips + jnp.arange(clips, dtype=jnp.int32)
    select = (clip_ids[:, None] == owned[None, :]).astype(jnp.float32)
    by_clip = jnp.einsum("ic,ifa->cfa", select, all_codes, precision=HIGHEST)
    codes_slot = jnp.einsum(
        "st,cta->csa", at_time.astype(jnp.float32), by_clip, precision=HIGHEST
    )
    action = jnp.einsum("csa,ad->csd", codes_slot, action_weight, precision=HIGHEST)

    spatial, own, mixed = [], [], None

    def add(mixed, j, late=()):
        back = [own[j] if m in late else arrived[j + AHEAD][m - 1] for m in range(1, n)]
        handed = arrived[j + 2 * AHEAD][0] if plan.slotted(j + AHEAD) else None
        return combine(
            plan, mixed, spatial[j], own[j], back, handed, projected, action, me, tables,
            j, width,
        )

    for j in range(count):
        for early in plan.chunks[len(spatial) : j + 2]:
            spatial.append(spatial_attention(projected, *early))
        ready = [*spatial, *own]
        done = temporal_attention(
            plan, projected, arrived[j], bias, action, after(me, *ready), tables, j
        )
        own.append(done[0])
        outgoing = done[1:]
        if j + 1 == count and n > max(LAST):
            outgoing = list(outgoing)
            for m, gates in LAST.items():
                outgoing[m - 1] = after(outgoing[m - 1], *[arrived[-1][g - 1] for g in gates])
        arrived.append(exchange(outgoing))
    last = count - 1
    start, heads = plan.chunks[last]
    split = n > max(LATE) and not plan.slotted(last + AHEAD) and start % heads == 0
    for j in range(count):
        mixed = add(mixed, j, LATE if split and j == last else ())
    if split:
        for m in LATE:
            mixed = add_rows(plan, mixed, spatial[last], arrived[last + AHEAD][m - 1], me, last, m)
    return mixed


def solution(mesh):
    return jax.shard_map(
        functools.partial(local, mesh.shape["frame"]),
        mesh=mesh,
        in_specs=(
            P(None, "dp", "frame", None, "mp"),
            P("dp", None, None),
            P(None, "mp"),
            P(),
            P(),
            P("dp", None),
        ),
        out_specs=P("dp", "frame", None, "mp"),
        check_vma=False,
    )
```
